256 devices in a mesh: dp: 256 (over y, x, z, core).
Axes of the slice: x: 4, y: 4, z: 8, core: 2. Of those that a mesh axis runs over, the one named last changes fastest.
Arguments:
- inputs: bfloat16 [65536, 4096], P('dp'), may hold values from -6 to 6
- out_grads: bfloat16 [65536, 512], P('dp'), may hold values from -6 to 6
- feedback: bfloat16 [1048576, 512], P('dp'), may hold values from -4 to 4
- q_start: float32 [512, 64], replicated, may hold values from -6 to 6
Outputs:
- update: float32 [4096, 512], P('dp')
- q_next: float32 [512, 64], replicated
- new_feedback: bfloat16 [1048576, 512], P('dp')
The draws below stay inside these ranges and needn't reach their ends.
All inputs are finite; a program needn't handle non-finite values.
Results may differ from the reference program's by a relative error of at most 0.001.
Values sent between devices are 32-bit elements; how exact they have to be, the bound alone decides.
A program may use at most 64 MiB of HBM per device.

```python
import jax
import jax.numpy as jnp
from jax import lax

D = 4096
KV = 512
RANK = 64
TOK_DEV = 256
TOKENS = 65536
EROWS = 1048576
N_DP = 256


def steps_of(key, dims, cuts, low, largest):
    level, own = 1.0, jax.random.fold_in(key, 6)
    for axis_at, blocks in cuts:
        heights = jnp.exp(jax.random.uniform(jax.random.fold_in(own, axis_at), (blocks,), jnp.float32, low / len(cuts), largest / len(cuts)))
        level = level * jnp.repeat(heights, dims[axis_at] // blocks).reshape([-1 if axis == axis_at else 1 for axis in range(len(dims))])
    return level


def bell_draw(own_key, extent, width, most, cuts=(), dtype=jnp.bfloat16):
    drawn = jax.random.normal(own_key, extent, jnp.float32) * width
    if len(cuts) > 0:
        drawn = steps_of(own_key, extent, cuts, -0.22, 0.18) * drawn
    return jnp.clip(drawn, min=-most, max=most).astype(dtype)


def setup_inputs(seed: int = 0) -> dict:
    arg_keys = jax.random.split(jax.random.key(seed), 5)
    return {
        "inputs": bell_draw(arg_keys[0], (TOKENS, D), 1.0, 6.0, ((0, 256),)),
        "out_grads": bell_draw(arg_keys[1], (TOKENS, KV), 1.0, 6.0, ((0, 256),)),
        "feedback": bell_draw(arg_keys[2], (EROWS, KV), 0.5, 4.0, ((0, 256),)),
        "q_start": bell_draw(arg_keys[3], (KV, RANK), 1.0, 6.0, (), jnp.float32),
    }


HIGH = lax.Precision.HIGHEST

def replica_matrix(x_rows, g_rows, fb_rows):
    grad = jnp.dot(x_rows.T.astype(jnp.float32), g_rows.astype(jnp.float32), preferred_element_type=jnp.float32)
    return grad * (1.0 / jnp.sqrt(jnp.float32(TOK_DEV))) + fb_rows.astype(jnp.float32)

def reference(inputs, out_grads, feedback, q_start):
    xs = inputs.reshape(N_DP, TOK_DEV, D)
    gs = out_grads.reshape(N_DP, TOK_DEV, KV)
    fbs = feedback.reshape(N_DP, D, KV)

    def add_p(total, item):
        matrix = replica_matrix(item[0], item[1], item[2])
        return (total + jnp.dot(matrix, q_start, precision=HIGH), None)
    p_sum, _ = lax.scan(add_p, jnp.zeros((D, RANK), jnp.float32), (xs, gs, fbs))
    gram = jnp.dot(p_sum.T, p_sum, precision=HIGH)
    lower = jnp.linalg.cholesky(gram)
    p_orth = jax.scipy.linalg.solve_triangular(lower, p_sum.T, lower=True).T

    def add_q(total, item):
        matrix = replica_matrix(item[0], item[1], item[2])
        return (total + jnp.dot(matrix.T, p_orth, precision=HIGH), None)
    q_sum, _ = lax.scan(add_q, jnp.zeros((KV, RANK), jnp.float32), (xs, gs, fbs))
    q_next = q_sum / jnp.float32(N_DP)
    update = jnp.dot(p_orth, q_next.T, precision=HIGH)

    def make_fb(item):
        matrix = replica_matrix(item[0], item[1], item[2])
        return (matrix - update).astype(jnp.bfloat16)
    new_fb = lax.map(make_fb, (xs, gs, fbs))
    return (update, q_next, new_fb.reshape(N_DP * D, KV))
```

```python
import jax
import jax.numpy as jnp
from jax import lax
from jax.experimental import pallas as pl
from jax.experimental.pallas import tpu as pltpu
from jax.sharding import PartitionSpec as P

HIGH = lax.Precision.HIGHEST
MESH = pl.DeviceIdType.MESH
F32, BF16 = jnp.float32, jnp.bfloat16

D, KV, RANK, TOK, N_DP = 4096, 512, 64, 256, 256
CH = 512
PLANE = [(dy, dx) for dy in range(4) for dx in range(4) if (dy, dx) != (0, 0)]


def nn(a, b):
    return lax.dot_general(a, b, (((1,), (0,)), ((), ())), preferred_element_type=F32)


def nt(a, b):
    return lax.dot_general(a, b, (((1,), (1,)), ((), ())), preferred_element_type=F32)


def tn(a, b):
    return lax.dot_general(a, b, (((0,), (0,)), ((), ())), preferred_element_type=F32)


def split(v, pieces):
    out = []
    for at in range(pieces):
        out.append(v.astype(BF16))
        if at < pieces - 1:
            v = v - out[-1].astype(F32)
    return out


def fold(t):
    return (t[128:192] + t[64:128]) + t[0:64]


def eliminate(a, first, last):
    rows = lax.broadcasted_iota(jnp.int32, (RANK, 1), 0)
    for k in range(first, last):
        row = a[k : k + 1, :]
        ratio = a[:, k : k + 1] / a[k : k + 1, k : k + 1]
        a = a - jnp.where(rows > k, ratio, 0.0) * row
    return a


def kernel(
    x_hbm, g_hbm, f_hbm, q_hbm, upd_ref, qn_ref, out_hbm,
    x_v, g_v, f_v, q_v, m_v, out_v, pt_v, p_full,
    core_send, core_recv, acc, plane_recv, z_send, z_recv,
    gram_v, st_v, y_v, s_send, s_recv, s_part, s_group, s_full,
    load_sem, x_sem, f_sem, out_sem,
    core_ss, core_rs, plane_ss, plane_rs, z_ss, z_rs,
    zg_ss, zg_rs, pg_ss, pg_rs, cg_ss, cg_rs,
    s1_ss, s1_rs, s2_ss, s2_rs, s3_ss, s3_rs,
):
    me = lax.axis_index("dp")
    core = lax.rem(me, 2)
    z = lax.rem(lax.div(me, 2), 8)
    group = lax.rem(me, 16)
    plane = lax.div(me, 16)
    y, x = lax.div(plane, 4), lax.rem(plane, 4)
    partner = me + 1 - 2 * core
    block = core * 16 + plane

    def plane_peer(dy, dx):
        return (lax.rem(y + dy, 4) * 4 + lax.rem(x + dx, 4)) * 16 + group

    def z_peer(dz):
        return plane * 16 + lax.rem(z + dz, 8) * 2 + core

    def group_peer(d):
        return plane * 16 + lax.rem(group + d, 16)

    def send(src, dst, ss, rs, device):
        copy = pltpu.make_async_remote_copy(
            src_ref=src, dst_ref=dst, send_sem=ss, recv_sem=rs,
            device_id=(device,), device_id_type=MESH,
        )
        copy.start()
        return copy

    started = []

    order = [lax.rem(y + t + 1, 4) for t in range(4)]
    chunks = [(1 - core) * 4 + c for c in order] + [core * 4 + c for c in order]
    loads = [
        pltpu.make_async_copy(q_hbm, q_v, load_sem.at[0]),
        pltpu.make_async_copy(g_hbm, g_v, load_sem.at[1]),
    ]
    for copy in loads:
        copy.start()
    x_loads, f_loads = [], []
    for i, c in enumerate(chunks):
        at = pl.ds(pl.multiple_of(c * CH, CH), CH)
        f_loads.append(pltpu.make_async_copy(f_hbm.at[at, :], f_v.at[at, :], f_sem.at[i]))
        x_loads.append(pltpu.make_async_copy(x_hbm.at[:, at], x_v.at[:, at], x_sem.at[i]))
        f_loads[-1].start()
        x_loads[-1].start()

    barrier = pltpu.get_barrier_semaphore()
    for dy, dx in PLANE:
        pl.semaphore_signal(barrier, inc=1, device_id=(plane_peer(dy, dx),), device_id_type=MESH)
    for d in range(1, 16):
        pl.semaphore_signal(barrier, inc=1, device_id=(group_peer(d),), device_id_type=MESH)

    for copy in loads:
        copy.wait()
    q3 = jnp.concatenate(split(q_v[...].T, 3), axis=0)
    gq3 = jnp.concatenate(split(fold(nt(q3, g_v[...])) * (1.0 / 16.0), 3), axis=0)

    def part(i):
        f_loads[i].wait()
        x_loads[i].wait()
        at = pl.ds(pl.multiple_of(chunks[i] * CH, CH), CH)
        return fold(nt(q3, f_v[at, :]) + nn(gq3, x_v[:, at]))

    core_copies = []
    for t in range(4):
        v = part(t)
        for i in range(4):
            core_send[t * 4 + i] = v[:, i * 128 : (i + 1) * 128]
        if t == 0:
            pl.semaphore_wait(barrier, 30)
        at = pl.ds(t * 4, 4)
        core_copies.append(send(core_send.at[at], core_recv.at[at], core_ss.at[t], core_rs.at[t], partner))
    plane_copies = {}
    for t in range(4):
        v = part(4 + t)
        core_copies[t].wait_recv()
        for i in range(4):
            acc[t * 4 + i] = v[:, i * 128 : (i + 1) * 128] + core_recv[t * 4 + i]
        dy = (t + 1) % 4
        for dx in range(4):
            d = dy * 4 + dx
            if d == 0:
                continue
            plane_copies[d] = send(
                acc.at[t * 4 + lax.rem(x + dx, 4)], plane_recv.at[d],
                plane_ss.at[d], plane_rs.at[d], plane_peer(dy, dx),
            )
    started += core_copies + list(plane_copies.values())

    def matrix(i, carry):
        at = pl.ds(pl.multiple_of(i * 256, 256), 256)
        m_v[at, :] = tn(x_v[:, at], g_v[...]) * (1.0 / 16.0) + f_v[at, :].astype(F32)
        return carry

    lax.fori_loop(0, D // 256, matrix, 0)

    s = acc[12 + x]
    for d in range(1, 16):
        plane_copies[d].wait_recv()
        s = s + plane_recv[d]
    for k in range(8):
        z_send[k] = s[k * 8 : (k + 1) * 8]
    z_copies = {}
    for dz in range(1, 8):
        z_copies[dz] = send(
            z_send.at[lax.rem(z + dz, 8)], z_recv.at[dz], z_ss.at[dz], z_rs.at[dz], z_peer(dz)
        )
    s = z_send[z]
    for dz in range(1, 8):
        z_copies[dz].wait_recv()
        s = s + z_recv[dz]
    p_full[block, z] = s
    started += list(z_copies.values())

    own = p_full.at[block, z]
    z_gathers = [send(own, own, zg_ss.at[dz], zg_rs.at[dz], z_peer(dz)) for dz in range(1, 8)]
    for copy in z_gathers:
        copy.wait_recv()
    mine = p_full.at[block]
    plane_gathers = {}
    for dy, dx in PLANE:
        d = dy * 4 + dx
        plane_gathers[d] = send(mine, mine, pg_ss.at[d], pg_rs.at[d], plane_peer(dy, dx))
    started += z_gathers + list(plane_gathers.values())

    def consume(c, first):
        p = p_full[pl.ds(c * 4, 4)].reshape(4, RANK, 128)
        p = jnp.concatenate([p[i] for i in range(4)], axis=1)
        p1, p2, p3 = split(p, 3)
        p3 = jnp.concatenate([p1, p2, p3], axis=0)
        at = pl.ds(pl.multiple_of(c * CH, CH), CH)
        gram, yt, st = nt(p3, p3), nt(p3, x_v[:, at]), nn(p3, f_v[at, :])
        gram_v[...] = gram if first else gram_v[...] + gram
        y_v[...] = yt if first else y_v[...] + yt
        st_v[...] = st if first else st_v[...] + st
        pt_v[at, :] = p3[0:128].T

    core_gathers = []
    for dy in range(4):
        for dx in range(4):
            if dy * 4 + dx > 0:
                plane_gathers[dy * 4 + dx].wait_recv()
        c = core * 4 + lax.rem(y + 4 - dy, 4)
        rows = p_full.at[pl.ds(c * 4, 4)]
        core_gathers.append(send(rows, rows, cg_ss.at[dy], cg_rs.at[dy], partner))
        consume(c, dy == 0)
    for dy in range(4):
        core_gathers[dy].wait_recv()
        consume((1 - core) * 4 + lax.rem(y + 4 - dy, 4), False)
    started += core_gathers

    y3 = jnp.concatenate(split(fold(y_v[...]) * (1.0 / 16.0), 3), axis=0)
    s = fold(st_v[...] + nn(y3, g_v[...]))
    for p in range(16):
        s_send[p] = s[(p // 2) * 8 : (p // 2) * 8 + 8, (p % 2) * 256 : (p % 2) * 256 + 256]
    s1 = {}
    for dy, dx in PLANE:
        d = dy * 4 + dx
        to = lax.rem(y + dy, 4) * 4 + lax.rem(x + dx, 4)
        s1[d] = send(s_send.at[to], s_recv.at[d], s1_ss.at[d], s1_rs.at[d], plane_peer(dy, dx))

    gram = gram_v[...]
    gram = fold(gram)
    gram = (gram[:, 128:192] + gram[:, 64:128]) + gram[:, 0:64]
    rows = lax.broadcasted_iota(jnp.int32, (RANK, RANK), 0)
    cols = lax.broadcasted_iota(jnp.int32, (RANK, RANK), 1)
    eye = (rows == cols).astype(F32)
    a = jnp.concatenate([gram, eye], axis=1)
    a = eliminate(a, 0, 22)

    s = s_send[plane]
    for d in range(1, 16):
        s1[d].wait_recv()
        s = s + s_recv[d]
    s_part[...] = s
    s_group[group] = s
    s2 = []
    for d in range(1, 16):
        s2.append(send(s_part, s_group.at[group], s2_ss.at[d], s2_rs.at[d], group_peer(d)))
    a = eliminate(a, 22, 43)
    for copy in s2:
        copy.wait_recv()
    s = s_group[0]
    for k in range(1, 16):
        s = s + s_group[k]
    s_full[plane] = s
    s3 = []
    for dy, dx in PLANE:
        d = dy * 4 + dx
        s3.append(send(s_full.at[plane], s_full.at[plane], s3_ss.at[d], s3_rs.at[d], plane_peer(dy, dx)))
    a = eliminate(a, 43, 64)
    diag = jnp.sum(a[:, 0:64] * eye, axis=1, keepdims=True)
    inv = a[:, 64:128] * (1.0 / jnp.sqrt(diag))
    inv_t = inv.T
    for copy in s3:
        copy.wait_recv()
    started += list(s1.values()) + s2 + s3

    s = jnp.concatenate(
        [jnp.concatenate([s_full[2 * r], s_full[2 * r + 1]], axis=1) for r in range(8)], axis=0
    )
    qn = jnp.dot(inv, s, precision=HIGH, preferred_element_type=F32) * (1.0 / N_DP)
    w = jnp.dot(inv_t, qn, precision=HIGH, preferred_element_type=F32)
    w1, w2 = split(w, 2)
    w = jnp.concatenate([w1, w1, w2, w2], axis=0)

    def finish(i, carry):
        at = pl.ds(pl.multiple_of(i * 256, 256), 256)
        p = pt_v[at, :]
        o = m_v[at, :] - nn(jnp.concatenate([p, p], axis=1), w)
        out_v[at, :] = o.astype(BF16)
        pltpu.make_async_copy(out_v.at[at, :], out_hbm.at[at, :], out_sem.at[i]).start()
        return carry

    lax.fori_loop(0, D // 256, finish, 0)
    p = pt_v[pl.ds(pl.multiple_of(me * 16, 16), 16), :]
    upd_ref[...] = nn(jnp.concatenate([p, p], axis=1), w)
    qn_ref[...] = qn.T
    for copy in started:
        copy.wait_send()

    def landed(i, carry):
        at = pl.ds(pl.multiple_of(i * 256, 256), 256)
        pltpu.make_async_copy(out_v.at[at, :], out_hbm.at[at, :], out_sem.at[i]).wait()
        return carry

    lax.fori_loop(0, D // 256, landed, 0)


def body(inputs, out_grads, feedback, q_start):
    dma = pltpu.SemaphoreType.DMA
    vmem = pltpu.VMEM
    return pl.pallas_call(
        kernel,
        out_shape=(
            jax.ShapeDtypeStruct((D // N_DP, KV), F32),
            jax.ShapeDtypeStruct((KV, RANK), F32),
            jax.ShapeDtypeStruct((D, KV), BF16),
        ),
        in_specs=[pl.BlockSpec(memory_space=pl.ANY)] * 4,
        out_specs=(
            pl.BlockSpec(memory_space=vmem),
            pl.BlockSpec(memory_space=vmem),
            pl.BlockSpec(memory_space=pl.ANY),
        ),
        scratch_shapes=[
            vmem((TOK, D), BF16),
            vmem((TOK, KV), BF16),
            vmem((D, KV), BF16),
            vmem((KV, RANK), F32),
            vmem((D, KV), F32),
            vmem((D, KV), BF16),
            vmem((D, 128), BF16),
            vmem((32, 8, 8, 128), F32),
            vmem((16, RANK, 128), F32),
            vmem((16, RANK, 128), F32),
            vmem((16, RANK, 128), F32),
            vmem((16, RANK, 128), F32),
            vmem((8, 8, 128), F32),
            vmem((8, 8, 128), F32),
            vmem((192, 192), F32),
            vmem((192, KV), F32),
            vmem((192, TOK), F32),
            vmem((16, 8, 256), F32),
            vmem((16, 8, 256), F32),
            vmem((8, 256), F32),
            vmem((16, 8, 256), F32),
            vmem((16, 8, 256), F32),
            dma((2,)), dma((8,)), dma((8,)), dma((16,)),
            dma((4,)), dma((4,)), dma((16,)), dma((16,)), dma((8,)), dma((8,)),
            dma((8,)), dma((8,)), dma((16,)), dma((16,)), dma((4,)), dma((4,)),
            dma((16,)), dma((16,)), dma((16,)), dma((16,)), dma((16,)), dma((16,)),
        ],
        compiler_params=pltpu.CompilerParams(
            collective_id=0, has_side_effects=True, vmem_limit_bytes=48 * 1024 * 1024
        ),
    )(inputs, out_grads, feedback, q_start)


def solution(mesh):
    placed = (P("dp", None), P("dp", None), P("dp", None), P())
    return jax.shard_map(
        body,
        mesh=mesh,
        in_specs=placed,
        out_specs=(P("dp", None), P(), P("dp", None)),
        check_vma=False,
    )
```

```python
import jax
import jax.numpy as jnp
from jax import lax
from jax.experimental import pallas as pl
from jax.experimental.pallas import tpu as pltpu
from jax.sharding import PartitionSpec as P

HIGH = lax.Precision.HIGHEST
MESH = pl.DeviceIdType.MESH
F32, BF16 = jnp.float32, jnp.bfloat16

D, KV, RANK, TOK, N_DP = 4096, 512, 64, 256, 256
CH = 512
HALF = RANK // 2
PLANE = [(dy, dx) for dy in range(4) for dx in range(4) if (dy, dx) != (0, 0)]
MIB = 1024 * 1024


def nn(a, b):
    return lax.dot_general(a, b, (((1,), (0,)), ((), ())), preferred_element_type=F32)


def nt(a, b):
    return lax.dot_general(a, b, (((1,), (1,)), ((), ())), preferred_element_type=F32)


def tn(a, b):
    return lax.dot_general(a, b, (((0,), (0,)), ((), ())), preferred_element_type=F32)


def split(v, pieces):
    out = []
    for at in range(pieces):
        out.append(v.astype(BF16))
        if at < pieces - 1:
            v = v - out[-1].astype(F32)
    return out


def fold(t):
    return (t[128:192] + t[64:128]) + t[0:64]


def eliminate(a, first, last):
    rows = lax.broadcasted_iota(jnp.int32, (RANK, 1), 0)
    for k in range(first, last):
        row = a[k : k + 1, :]
        ratio = a[:, k : k + 1] / a[k : k + 1, k : k + 1]
        a = a - jnp.where(rows > k, ratio, 0.0) * row
    return a


def kernel(
    x_hbm, g_hbm, f_hbm, q_hbm, upd_ref, qn_ref, m_ref, pt_ref, w_ref,
    x_v, g_v, f_v, q_v, p_full,
    terms, core_recv, acc, plane_recv, z_group,
    gram_v, st_v, y_v, s_send, s_recv, s_group, s_core, s_full,
    load_sem, x_sem, f_sem,
    core_ss, core_rs, plane_ss, plane_rs, z_ss, z_rs,
    pg_ss, pg_rs, cg_ss, cg_rs,
    s1_ss, s1_rs, s2_ss, s2_rs, sc_ss, sc_rs, s3_ss, s3_rs,
):
    me = lax.axis_index("dp")
    core = lax.rem(me, 2)
    z = lax.rem(lax.div(me, 2), 8)
    group = lax.rem(me, 16)
    plane = lax.div(me, 16)
    y, x = lax.div(plane, 4), lax.rem(plane, 4)
    partner = me + 1 - 2 * core
    own = pl.ds(pl.multiple_of(core * HALF, HALF), HALF)
    other = pl.ds(pl.multiple_of((1 - core) * HALF, HALF), HALF)

    def plane_peer(dy, dx):
        return (lax.rem(y + dy, 4) * 4 + lax.rem(x + dx, 4)) * 16 + group

    def z_peer(dz):
        return plane * 16 + lax.rem(z + dz, 8) * 2 + core

    started = []

    def send(src, dst, ss, rs, device):
        copy = pltpu.make_async_remote_copy(
            src_ref=src, dst_ref=dst, send_sem=ss, recv_sem=rs,
            device_id=(device,), device_id_type=MESH,
        )
        copy.start()
        started.append(copy)
        return copy

    order = [lax.rem(y + t + 1, 4) for t in range(4)]
    chunks = order + [4 + c for c in order]
    loads = [
        pltpu.make_async_copy(q_hbm, q_v, load_sem.at[0]),
        pltpu.make_async_copy(g_hbm, g_v, load_sem.at[1]),
    ]
    for copy in loads:
        copy.start()
    x_loads, f_loads = [], []
    for i, c in enumerate(chunks):
        at = pl.ds(pl.multiple_of(c * CH, CH), CH)
        f_loads.append(pltpu.make_async_copy(f_hbm.at[at, :], f_v.at[at, :], f_sem.at[i]))
        x_loads.append(pltpu.make_async_copy(x_hbm.at[:, at], x_v.at[:, at], x_sem.at[i]))
        f_loads[-1].start()
        x_loads[-1].start()

    barrier = pltpu.get_barrier_semaphore()
    for dy, dx in PLANE:
        pl.semaphore_signal(barrier, inc=1, device_id=(plane_peer(dy, dx),), device_id_type=MESH)
    for dz in range(1, 8):
        pl.semaphore_signal(barrier, inc=1, device_id=(z_peer(dz),), device_id_type=MESH)
    pl.semaphore_signal(barrier, inc=1, device_id=(partner,), device_id_type=MESH)

    for copy in loads:
        copy.wait()
    q3 = jnp.concatenate(split(q_v[...], 3), axis=0)
    gq3 = jnp.concatenate(split(fold(nt(q3, g_v[...])) * (1.0 / 16.0), 3), axis=0)

    def term(c):
        f_loads[c].wait()
        x_loads[c].wait()
        at = pl.ds(pl.multiple_of(chunks[c] * CH, CH), CH)
        v = fold(nt(q3, f_v[at, :]) + nn(gq3, x_v[:, at]))
        for i in range(4):
            terms[c * 4 + i] = v[:, i * 128 : (i + 1) * 128]

    core_copies, plane_copies = {}, {}

    def to_core(c):
        at = pl.ds(c * 4, 4)
        core_copies[c] = send(
            terms.at[at, other], core_recv.at[at], core_ss.at[c], core_rs.at[c], partner
        )

    def to_plane(c):
        core_copies[c].wait_recv()
        at = pl.ds(c * 4, 4)
        acc[at] = terms[at, own, :] + core_recv[at]
        part, dy = c // 4, (c % 4 + 1) % 4
        for dx in range(4):
            d = dy * 4 + dx
            if d > 0:
                plane_copies[part, d] = send(
                    acc.at[c * 4 + lax.rem(x + dx, 4)], plane_recv.at[part, d],
                    plane_ss.at[part, d], plane_rs.at[part, d], plane_peer(dy, dx),
                )

    for c in range(4):
        term(c)
    pl.semaphore_wait(barrier, 23)
    for c in range(4):
        to_core(c)
    for c in range(4, 8):
        term(c)
        to_core(c)
        if c >= 5:
            to_plane(c - 5)
    for c in range(3, 8):
        to_plane(c)

    def matrix(i, carry):
        at = pl.ds(pl.multiple_of(i * CH, CH), CH)
        m_ref[at, :] = tn(x_v[:, at], g_v[...]) * (1.0 / 16.0) + f_v[at, :].astype(F32)
        return carry

    lax.fori_loop(0, D // CH, matrix, 0)

    z_copies = []
    for part in range(2):
        s = acc[part * 16 + 12 + x]
        for d in range(1, 16):
            plane_copies[part, d].wait_recv()
            s = s + plane_recv[part, d]
        z_group[part, z] = s
        mine = z_group.at[part, z]
        z_copies.append(
            [send(mine, mine, z_ss.at[part, dz], z_rs.at[part, dz], z_peer(dz)) for dz in range(1, 8)]
        )

    plane_gathers = {}
    for part in range(2):
        for copy in z_copies[part]:
            copy.wait_recv()
        s = z_group[part, 0]
        for k in range(1, 8):
            s = s + z_group[part, k]
        p_full[part * 16 + plane, own, :] = s
        mine = p_full.at[part * 16 + plane, own]
        for dy, dx in PLANE:
            d = dy * 4 + dx
            plane_gathers[part, d] = send(
                mine, mine, pg_ss.at[part, d], pg_rs.at[part, d], plane_peer(dy, dx)
            )

    def consume(c, first):
        p = p_full[pl.ds(c * 4, 4)]
        p = jnp.concatenate([p[i] for i in range(4)], axis=1)
        p1, p2, p3 = split(p, 3)
        p3 = jnp.concatenate([p1, p2, p3], axis=0)
        at = pl.ds(pl.multiple_of(c * CH, CH), CH)
        gram, yt, st = nt(p3, p3), nt(p3, x_v[:, at]), nn(p3, f_v[at, :])
        gram_v[...] = gram if first else gram_v[...] + gram
        y_v[...] = yt if first else y_v[...] + yt
        st_v[...] = st if first else st_v[...] + st
        pt_ref[at, :] = p3[0:128].T

    for part in range(2):
        core_gathers = {}
        for dy in (0, 1, 3, 2):
            for dx in range(4):
                if dy * 4 + dx > 0:
                    plane_gathers[part, dy * 4 + dx].wait_recv()
            rows = p_full.at[pl.ds(part * 16 + lax.rem(y + 4 - dy, 4) * 4, 4), own]
            core_gathers[dy] = send(rows, rows, cg_ss.at[part, dy], cg_rs.at[part, dy], partner)
        for dy in (0, 1, 3, 2):
            core_gathers[dy].wait_recv()
            consume(part * 4 + lax.rem(y + 4 - dy, 4), part == 0 and dy == 0)

    y3 = jnp.concatenate(split(fold(y_v[...]) * (1.0 / 16.0), 3), axis=0)
    s = fold(st_v[...] + nn(y3, g_v[...]))
    for p in range(16):
        s_send[p] = s[(p // 2) * 8 : (p // 2) * 8 + 8, (p % 2) * 256 : (p % 2) * 256 + 256]
    s1 = {}
    for dy, dx in PLANE:
        d = dy * 4 + dx
        to = lax.rem(y + dy, 4) * 4 + lax.rem(x + dx, 4)
        s1[d] = send(s_send.at[to], s_recv.at[d], s1_ss.at[d], s1_rs.at[d], plane_peer(dy, dx))

    gram = gram_v[...]
    gram = fold(gram)
    gram = (gram[:, 128:192] + gram[:, 64:128]) + gram[:, 0:64]
    rows = lax.broadcasted_iota(jnp.int32, (RANK, RANK), 0)
    cols = lax.broadcasted_iota(jnp.int32, (RANK, RANK), 1)
    eye = (rows == cols).astype(F32)
    a = jnp.concatenate([gram, eye], axis=1)
    a = eliminate(a, 0, 22)

    s = s_send[plane]
    for d in range(1, 16):
        s1[d].wait_recv()
        s = s + s_recv[d]
    s_group[z] = s
    mine = s_group.at[z]
    s2 = [send(mine, mine, s2_ss.at[dz], s2_rs.at[dz], z_peer(dz)) for dz in range(1, 8)]
    a = eliminate(a, 22, 43)
    for copy in s2:
        copy.wait_recv()
    s = s_group[0]
    for k in range(1, 8):
        s = s + s_group[k]
    s_core[0] = s
    copy = send(s_core.at[0], s_core.at[1], sc_ss, sc_rs, partner)
    copy.wait_recv()
    s_full[plane] = s + s_core[1]
    mine = s_full.at[plane]
    s3 = []
    for dy, dx in PLANE:
        d = dy * 4 + dx
        s3.append(send(mine, mine, s3_ss.at[d], s3_rs.at[d], plane_peer(dy, dx)))
    a = eliminate(a, 43, 64)
    diag = jnp.sum(a[:, 0:64] * eye, axis=1, keepdims=True)
    inv = a[:, 64:128] * (1.0 / jnp.sqrt(diag))
    inv_t = inv.T
    for copy in s3:
        copy.wait_recv()

    s = jnp.concatenate(
        [jnp.concatenate([s_full[2 * r], s_full[2 * r + 1]], axis=1) for r in range(8)], axis=0
    )
    qn = jnp.dot(inv, s, precision=HIGH, preferred_element_type=F32) * (1.0 / N_DP)
    w = jnp.dot(inv_t, qn, precision=HIGH, preferred_element_type=F32)
    w1, w2 = split(w, 2)
    w = jnp.concatenate([w1, w1, w2, w2], axis=0)
    w_ref[...] = w
    qn_ref[...] = qn
    p = pt_ref[pl.ds(pl.multiple_of(me * 16, 16), 16), :]
    upd_ref[...] = nn(jnp.concatenate([p, p], axis=1), w)
    for copy in started:
        copy.wait_send()


def finish(upd_v, qn_v, m_v, pt_v, w_v, upd_hbm, qn_hbm, out_hbm, out_v, small_sem, out_sem):
    small = [
        pltpu.make_async_copy(upd_v, upd_hbm, small_sem.at[0]),
        pltpu.make_async_copy(qn_v, qn_hbm, small_sem.at[1]),
    ]
    for copy in small:
        copy.start()
    w = w_v[...]
    copies = []
    for i in range(D // CH):
        at = pl.ds(i * CH, CH)
        p = pt_v[at, :]
        out_v[at, :] = (m_v[at, :] - nn(jnp.concatenate([p, p], axis=1), w)).astype(BF16)
        copies.append(pltpu.make_async_copy(out_v.at[at, :], out_hbm.at[at, :], out_sem.at[i]))
        copies[-1].start()
    for copy in small + copies:
        copy.wait()


def body(inputs, out_grads, feedback, q_start):
    dma = pltpu.SemaphoreType.DMA
    vmem = pltpu.VMEM
    in_vmem = pl.BlockSpec(memory_space=vmem)
    in_any = pl.BlockSpec(memory_space=pl.ANY)
    upd, qn, m, pt, w = pl.pallas_call(
        kernel,
        out_shape=(
            vmem((D // N_DP, KV), F32),
            vmem((RANK, KV), F32),
            vmem((D, KV), F32),
            vmem((D, 128), BF16),
            vmem((256, KV), BF16),
        ),
        in_specs=[in_any] * 4,
        out_specs=(in_vmem,) * 5,
        scratch_shapes=[
            vmem((TOK, D), BF16),
            vmem((TOK, KV), BF16),
            vmem((D, KV), BF16),
            vmem((RANK, KV), F32),
            vmem((32, RANK, 128), F32),
            vmem((32, RANK, 128), F32),
            vmem((32, HALF, 128), F32),
            vmem((32, HALF, 128), F32),
            vmem((2, 16, HALF, 128), F32),
            vmem((2, 8, HALF, 128), F32),
            vmem((192, 192), F32),
            vmem((192, KV), F32),
            vmem((192, TOK), F32),
            vmem((16, 8, 256), F32),
            vmem((16, 8, 256), F32),
            vmem((8, 8, 256), F32),
            vmem((2, 8, 256), F32),
            vmem((16, 8, 256), F32),
            dma((2,)), dma((8,)), dma((8,)),
            dma((8,)), dma((8,)), dma((2, 16)), dma((2, 16)), dma((2, 8)), dma((2, 8)),
            dma((2, 16)), dma((2, 16)), dma((2, 4)), dma((2, 4)),
            dma((16,)), dma((16,)), dma((8,)), dma((8,)), dma, dma, dma((16,)), dma((16,)),
        ],
        compiler_params=pltpu.CompilerParams(
            collective_id=0, has_side_effects=True, vmem_limit_bytes=52 * MIB
        ),
    )(inputs, out_grads, feedback, q_start.T)
    upd, qn, new_feedback = pl.pallas_call(
        finish,
        out_shape=(
            jax.ShapeDtypeStruct((D // N_DP, KV), F32),
            jax.ShapeDtypeStruct((RANK, KV), F32),
            jax.ShapeDtypeStruct((D, KV), BF16),
        ),
        in_specs=[in_vmem] * 5,
        out_specs=(in_any,) * 3,
        scratch_shapes=[vmem((D, KV), BF16), dma((2,)), dma((8,))],
        compiler_params=pltpu.CompilerParams(vmem_limit_bytes=16 * MIB),
    )(upd, qn, m, pt, w)
    return upd, qn.T, new_feedback


def solution(mesh):
    placed = (P("dp", None), P("dp", None), P("dp", None), P())
    return jax.shard_map(
        body,
        mesh=mesh,
        in_specs=placed,
        out_specs=(P("dp", None), P(), P("dp", None)),
        check_vma=False,
    )
```

```python
import jax
import jax.numpy as jnp
from jax import lax
from jax.experimental import pallas as pl
from jax.experimental.pallas import tpu as pltpu
from jax.sharding import PartitionSpec as P

HIGH = lax.Precision.HIGHEST
MESH = pl.DeviceIdType.MESH
F32, BF16 = jnp.float32, jnp.bfloat16

D, KV, RANK, TOK, N_DP = 4096, 512, 64, 256, 256
HALF = RANK // 2
CH = 512
PARTS = 4
PART = D // PARTS
BLOCKS = PART // 128
ROWS = HALF // 2
PLANE = [(dy, dx) for dy in range(4) for dx in range(4) if (dy, dx) != (0, 0)]
MIB = 1024 * 1024


def nn(a, b):
    return lax.dot_general(a, b, (((1,), (0,)), ((), ())), preferred_element_type=F32)


def nt(a, b):
    return lax.dot_general(a, b, (((1,), (1,)), ((), ())), preferred_element_type=F32)


def tn(a, b):
    return lax.dot_general(a, b, (((0,), (0,)), ((), ())), preferred_element_type=F32)


def split(v, pieces):
    out = []
    for at in range(pieces):
        out.append(v.astype(BF16))
        if at < pieces - 1:
            v = v - out[-1].astype(F32)
    return out


def fold(t):
    out = t[-RANK:]
    for at in range(t.shape[0] - 2 * RANK, -1, -RANK):
        out = out + t[at : at + RANK]
    return out


def eliminate(a, first, last):
    rows = lax.broadcasted_iota(jnp.int32, (RANK, 1), 0)
    for k in range(first, last):
        row = a[k : k + 1, :]
        ratio = a[:, k : k + 1] / a[k : k + 1, k : k + 1]
        a = a - jnp.where(rows > k, ratio, 0.0) * row
    return a


def kernel(
    x_hbm, g_hbm, f_hbm, q_hbm, upd_ref, qn_ref, m_ref, pt_ref, w_ref,
    x_v, g_v, f_v, q_v, p_full,
    terms, core_recv, acc, plane_recv, z_group,
    st_v, y_v, s_send, s_recv, s_group, s_core, s_full,
    load_sem, send_sem, core_sem, plane_sem, z_sem, gather_sem, pair_sem, s_sem,
):
    me = lax.axis_index("dp")
    core = lax.rem(me, 2)
    z = lax.rem(lax.div(me, 2), 8)
    group = lax.rem(me, 16)
    plane = lax.div(me, 16)
    y, x = lax.div(plane, 4), lax.rem(plane, 4)
    partner = me + 1 - 2 * core
    own = pl.ds(pl.multiple_of(core * HALF, HALF), HALF)
    other = pl.ds(pl.multiple_of((1 - core) * HALF, HALF), HALF)

    def place(dy, dx):
        return lax.rem(y + dy, 4) * 4 + lax.rem(x + dx, 4)

    def plane_peer(dy, dx):
        return place(dy, dx) * 16 + group

    def z_peer(dz):
        return plane * 16 + lax.rem(z + dz, 8) * 2 + core

    def send(src, dst, ss, rs, device):
        pltpu.make_async_remote_copy(
            src_ref=src, dst_ref=dst, send_sem=ss, recv_sem=rs,
            device_id=(device,), device_id_type=MESH,
        ).start()

    def take(like, sem):
        pltpu.make_async_copy(like, like, sem).wait()

    loads = [
        pltpu.make_async_copy(q_hbm, q_v, load_sem.at[0]),
        pltpu.make_async_copy(g_hbm, g_v, load_sem.at[1]),
    ]
    for part in range(PARTS):
        at = pl.ds(part * PART, PART)
        loads.append(pltpu.make_async_copy(f_hbm.at[at, :], f_v.at[at, :], load_sem.at[2 + 2 * part]))
        loads.append(pltpu.make_async_copy(x_hbm.at[:, at], x_v.at[:, at], load_sem.at[3 + 2 * part]))
    for copy in loads:
        copy.start()

    barrier = pltpu.get_barrier_semaphore()
    for dy, dx in PLANE:
        pl.semaphore_signal(barrier, inc=1, device_id=(plane_peer(dy, dx),), device_id_type=MESH)
    for dz in range(1, 8):
        pl.semaphore_signal(barrier, inc=1, device_id=(z_peer(dz),), device_id_type=MESH)
    pl.semaphore_signal(barrier, inc=1, device_id=(partner,), device_id_type=MESH)

    for copy in loads[0:2]:
        copy.wait()
    q2 = jnp.concatenate(split(q_v[...], 2), axis=0)
    gq2 = jnp.concatenate(split(fold(nt(q2, g_v[...])) * (1.0 / 16.0), 2), axis=0)

    def term(part):
        for copy in loads[2 + 2 * part : 4 + 2 * part]:
            copy.wait()
        for c in range(part * PART // CH, (part + 1) * PART // CH):
            at = pl.ds(c * CH, CH)
            v = fold(nt(q2, f_v[at, :]) + nn(gq2, x_v[:, at]))
            for i in range(4):
                terms[c * 4 + i] = v[:, i * 128 : (i + 1) * 128]

    def to_core(part):
        at = pl.ds(part * BLOCKS, BLOCKS)
        send(terms.at[at, other], core_recv.at[at], send_sem.at[0], core_sem.at[part], partner)

    def piece(part, to):
        return part * BLOCKS + lax.div(to, 2), pl.ds(pl.multiple_of(lax.rem(to, 2) * ROWS, ROWS), ROWS)

    def to_plane(part):
        at = pl.ds(part * BLOCKS, BLOCKS)
        take(core_recv.at[at], core_sem.at[part])
        acc[at] = terms[at, own, :] + core_recv[at]
        for dy, dx in PLANE:
            send(
                acc.at[piece(part, place(dy, dx))], plane_recv.at[part, dy * 4 + dx],
                send_sem.at[1], plane_sem.at[part], plane_peer(dy, dx),
            )

    term(0)
    term(1)
    pl.semaphore_wait(barrier, 23)
    to_core(0)
    to_core(1)
    term(2)
    to_core(2)
    to_plane(0)
    term(3)
    to_core(3)
    for part in range(1, PARTS):
        to_plane(part)

    for c in range(D // CH):
        at = pl.ds(c * CH, CH)
        m_ref[at, :] = tn(x_v[:, at], g_v[...]) * (1.0 / 16.0) + f_v[at, :].astype(F32)

    for part in range(PARTS):
        if part == 3:
            pass
        take(plane_recv.at[part, pl.ds(1, 15)], plane_sem.at[part])
        block, rows = piece(part, plane)
        s = acc[block, rows, :]
        for d in range(1, 16):
            s = s + plane_recv[part, d]
        z_group[part, z] = s
        mine = z_group.at[part, z]
        for dz in range(1, 8):
            send(mine, mine, send_sem.at[2], z_sem.at[part], z_peer(dz))

    for part in range(PARTS):
        if part == 3:
            pass
        take(z_group.at[part, pl.ds(0, 7)], z_sem.at[part])
        s = z_group[part, 0]
        for k in range(1, 8):
            s = s + z_group[part, k]
        block = part * BLOCKS + lax.div(plane, 2)
        rows = pl.ds(pl.multiple_of(core * HALF + lax.rem(plane, 2) * ROWS, ROWS), ROWS)
        p_full[block, rows, :] = s
        mine = p_full.at[block, rows]
        for dy, dx in PLANE:
            send(mine, mine, send_sem.at[3], gather_sem.at[part], plane_peer(dy, dx))

    def pieces(c, count):
        p = p_full[pl.ds(c * 4, 4)]
        p = jnp.concatenate([p[i] for i in range(4)], axis=1)
        return jnp.concatenate(split(p, count), axis=0)

    def consume(part):
        yt, st = [], []
        for c in range(part * PART // CH, (part + 1) * PART // CH):
            p2 = pieces(c, 2)
            at = pl.ds(c * CH, CH)
            yt.append(nt(p2, x_v[:, at]))
            st.append(nn(p2, f_v[at, :]))
        yt, st = sum(yt[1:], yt[0]), sum(st[1:], st[0])
        y_v[...] = yt if part == 0 else y_v[...] + yt
        st_v[...] = st if part == 0 else st_v[...] + st

    for part in range(PARTS):
        if part == 3:
            pass
        take(plane_recv.at[part, pl.ds(1, 15)], gather_sem.at[part])
        rows = p_full.at[pl.ds(part * BLOCKS, BLOCKS), own]
        send(rows, rows, send_sem.at[4], pair_sem.at[part], partner)
        take(rows, pair_sem.at[part])
        consume(part)

    y2 = jnp.concatenate(split(fold(y_v[...]) * (1.0 / 16.0), 2), axis=0)
    s = fold(st_v[...] + nn(y2, g_v[...]))
    for p in range(16):
        s_send[p] = s[(p // 2) * 8 : (p // 2) * 8 + 8, (p % 2) * 256 : (p % 2) * 256 + 256]
    for dy, dx in PLANE:
        send(
            s_send.at[place(dy, dx)], s_recv.at[dy * 4 + dx],
            send_sem.at[5], s_sem.at[0], plane_peer(dy, dx),
        )

    gram = jnp.zeros((3 * RANK, 3 * RANK), F32)
    for c in range(8):
        p3 = pieces(c, 3)
        gram = gram + nt(p3, p3)
        pt_ref[c * CH : (c + 1) * CH, :] = p3[0:128].T
    gram = fold(gram)
    gram = (gram[:, 128:192] + gram[:, 64:128]) + gram[:, 0:64]
    rows = lax.broadcasted_iota(jnp.int32, (RANK, RANK), 0)
    cols = lax.broadcasted_iota(jnp.int32, (RANK, RANK), 1)
    eye = (rows == cols).astype(F32)
    a = jnp.concatenate([gram, eye], axis=1)
    a = eliminate(a, 0, 22)

    take(s_recv.at[pl.ds(1, 15)], s_sem.at[0])
    s = s_send[plane]
    for d in range(1, 16):
        s = s + s_recv[d]
    s_group[z] = s
    mine = s_group.at[z]
    for dz in range(1, 8):
        send(mine, mine, send_sem.at[6], s_sem.at[1], z_peer(dz))
    a = eliminate(a, 22, 43)
    take(s_group.at[pl.ds(0, 7)], s_sem.at[1])
    s = s_group[0]
    for k in range(1, 8):
        s = s + s_group[k]
    s_core[0] = s
    send(s_core.at[0], s_core.at[1], send_sem.at[7], s_sem.at[2], partner)
    take(s_core.at[1], s_sem.at[2])
    s_full[plane] = s + s_core[1]
    mine = s_full.at[plane]
    for dy, dx in PLANE:
        send(mine, mine, send_sem.at[8], s_sem.at[3], plane_peer(dy, dx))
    a = eliminate(a, 43, 64)
    diag = jnp.sum(a[:, 0:64] * eye, axis=1, keepdims=True)
    inv = a[:, 64:128] * (1.0 / jnp.sqrt(diag))
    inv_t = inv.T
    take(core_recv, send_sem.at[0])
    take(plane_recv.at[:, pl.ds(1, 15)], send_sem.at[1])
    take(z_group.at[:, pl.ds(0, 7)], send_sem.at[2])
    take(plane_recv.at[:, pl.ds(1, 15)], send_sem.at[3])
    take(core_recv, send_sem.at[4])
    take(s_recv.at[pl.ds(1, 15)], send_sem.at[5])
    take(s_group.at[pl.ds(0, 7)], send_sem.at[6])
    take(s_core.at[1], send_sem.at[7])
    take(s_recv.at[pl.ds(1, 15)], s_sem.at[3])

    s = jnp.concatenate(
        [jnp.concatenate([s_full[2 * r], s_full[2 * r + 1]], axis=1) for r in range(8)], axis=0
    )
    qn = jnp.dot(inv, s, precision=HIGH, preferred_element_type=F32) * (1.0 / N_DP)
    w = jnp.dot(inv_t, qn, precision=HIGH, preferred_element_type=F32)
    w1, w2 = split(w, 2)
    w = jnp.concatenate([w1, w1, w2, w2], axis=0)
    w_ref[...] = w
    qn_ref[...] = qn
    p = pt_ref[pl.ds(pl.multiple_of(me * 16, 16), 16), :]
    upd_ref[...] = nn(jnp.concatenate([p, p], axis=1), w)
    take(s_recv.at[pl.ds(1, 15)], send_sem.at[8])


def finish(upd_v, qn_v, m_v, pt_v, w_v, upd_hbm, qn_hbm, out_hbm, out_v, small_sem):
    small = [
        pltpu.make_async_copy(upd_v, upd_hbm, small_sem.at[0]),
        pltpu.make_async_copy(qn_v, qn_hbm, small_sem.at[1]),
    ]
    for copy in small:
        copy.start()
    w = w_v[...]
    for i in range(D // CH):
        at = pl.ds(i * CH, CH)
        p = pt_v[at, :]
        out_v[at, :] = (m_v[at, :] - nn(jnp.concatenate([p, p], axis=1), w)).astype(BF16)
        pltpu.make_async_copy(out_v.at[at, :], out_hbm.at[at, :], small_sem.at[2]).start()
    for copy in small:
        copy.wait()
    pltpu.make_async_copy(out_v, out_hbm, small_sem.at[2]).wait()


def body(inputs, out_grads, feedback, q_start):
    dma = pltpu.SemaphoreType.DMA
    vmem = pltpu.VMEM
    in_vmem = pl.BlockSpec(memory_space=vmem)
    in_any = pl.BlockSpec(memory_space=pl.ANY)
    upd, qn, m, pt, w = pl.pallas_call(
        kernel,
        out_shape=(
            vmem((D // N_DP, KV), F32),
            vmem((RANK, KV), F32),
            vmem((D, KV), F32),
            vmem((D, 128), BF16),
            vmem((256, KV), BF16),
        ),
        in_specs=[in_any] * 4,
        out_specs=(in_vmem,) * 5,
        scratch_shapes=[
            vmem((TOK, D), BF16),
            vmem((TOK, KV), BF16),
            vmem((D, KV), BF16),
            vmem((RANK, KV), F32),
            vmem((32, RANK, 128), F32),
            vmem((32, RANK, 128), F32),
            vmem((32, HALF, 128), F32),
            vmem((32, HALF, 128), F32),
            vmem((PARTS, 16, ROWS, 128), F32),
            vmem((PARTS, 8, ROWS, 128), F32),
            vmem((2 * RANK, KV), F32),
            vmem((2 * RANK, TOK), F32),
            vmem((16, 8, 256), F32),
            vmem((16, 8, 256), F32),
            vmem((8, 8, 256), F32),
            vmem((2, 8, 256), F32),
            vmem((16, 8, 256), F32),
            dma((2 + 2 * PARTS,)), dma((9,)), dma((PARTS,)), dma((PARTS,)),
            dma((PARTS,)), dma((PARTS,)), dma((PARTS,)), dma((4,)),
        ],
        compiler_params=pltpu.CompilerParams(
            collective_id=0, has_side_effects=True, vmem_limit_bytes=52 * MIB
        ),
    )(inputs, out_grads, feedback, q_start.T)
    upd, qn, new_feedback = pl.pallas_call(
        finish,
        out_shape=(
            jax.ShapeDtypeStruct((D // N_DP, KV), F32),
            jax.ShapeDtypeStruct((RANK, KV), F32),
            jax.ShapeDtypeStruct((D, KV), BF16),
        ),
        in_specs=[in_vmem] * 5,
        out_specs=(in_any,) * 3,
        scratch_shapes=[vmem((D, KV), BF16), dma((3,))],
        compiler_params=pltpu.CompilerParams(vmem_limit_bytes=16 * MIB),
    )(upd, qn, m, pt, w)
    return upd, qn.T, new_feedback


def solution(mesh):
    placed = (P("dp", None), P("dp", None), P("dp", None), P())
    return jax.shard_map(
        body,
        mesh=mesh,
        in_specs=placed,
        out_specs=(P("dp", None), P(), P("dp", None)),
        check_vma=False,
    )
```

```python
import jax
import jax.numpy as jnp
from jax import lax
from jax.experimental import pallas as pl
from jax.experimental.pallas import tpu as pltpu
from jax.sharding import PartitionSpec as P

HIGH = lax.Precision.HIGHEST
MESH = pl.DeviceIdType.MESH
F32, BF16 = jnp.float32, jnp.bfloat16

D, KV, RANK, TOK, N_DP = 4096, 512, 64, 256, 256
HALF = RANK // 2
CH = 512
PARTS = 4
PART = D // PARTS
BLOCKS = PART // 128
ROWS = HALF // 2
PLANE = [(2, 2), (2, 1), (2, 3), (1, 2), (3, 2), (1, 1), (1, 3), (3, 1), (3, 3), (2, 0), (0, 2), (0, 1), (0, 3), (1, 0), (3, 0)]
MIB = 1024 * 1024


def nn(a, b):
    return lax.dot_general(a, b, (((1,), (0,)), ((), ())), preferred_element_type=F32)


def nt(a, b):
    return lax.dot_general(a, b, (((1,), (1,)), ((), ())), preferred_element_type=F32)


def tn(a, b):
    return lax.dot_general(a, b, (((0,), (0,)), ((), ())), preferred_element_type=F32)


def split(v, pieces):
    out = []
    for at in range(pieces):
        out.append(v.astype(BF16))
        if at < pieces - 1:
            v = v - out[-1].astype(F32)
    return out


def fold(t):
    out = t[-RANK:]
    for at in range(t.shape[0] - 2 * RANK, -1, -RANK):
        out = out + t[at : at + RANK]
    return out


def eliminate(a, first, last):
    rows = lax.broadcasted_iota(jnp.int32, (RANK, 1), 0)
    for k in range(first, last):
        row = a[k : k + 1, :]
        ratio = a[:, k : k + 1] / a[k : k + 1, k : k + 1]
        a = a - jnp.where(rows > k, ratio, 0.0) * row
    return a


def kernel(
    x_hbm, g_hbm, f_hbm, q_hbm, upd_ref, qn_ref, m_ref, pt_ref, w_ref,
    x_v, g_v, f_v, q_v, p_full,
    terms, core_recv, acc, plane_recv, z_group,
    m_peer, m_chip, st_v, s_send, s_recv, s_group, s_full,
    load_sem, send_sem, core_sem, plane_sem, z_sem, gather_sem, pair_sem, s_sem, peer_sem,
):
    me = lax.axis_index("dp")
    core = lax.rem(me, 2)
    z = lax.rem(lax.div(me, 2), 8)
    group = lax.rem(me, 16)
    plane = lax.div(me, 16)
    y, x = lax.div(plane, 4), lax.rem(plane, 4)
    partner = me + 1 - 2 * core
    own = pl.ds(pl.multiple_of(core * HALF, HALF), HALF)
    other = pl.ds(pl.multiple_of((1 - core) * HALF, HALF), HALF)

    def place(dy, dx):
        return lax.rem(y + dy, 4) * 4 + lax.rem(x + dx, 4)

    def plane_peer(dy, dx):
        return place(dy, dx) * 16 + group

    def z_peer(dz):
        return plane * 16 + lax.rem(z + dz, 8) * 2 + core

    def send(src, dst, ss, rs, device):
        pltpu.make_async_remote_copy(
            src_ref=src, dst_ref=dst, send_sem=ss, recv_sem=rs,
            device_id=(device,), device_id_type=MESH,
        ).start()

    def take(like, sem):
        pltpu.make_async_copy(like, like, sem).wait()

    loads = [
        pltpu.make_async_copy(q_hbm, q_v, load_sem.at[0]),
        pltpu.make_async_copy(g_hbm, g_v, load_sem.at[1]),
    ]
    for part in range(PARTS):
        at = pl.ds(part * PART, PART)
        loads.append(pltpu.make_async_copy(f_hbm.at[at, :], f_v.at[at, :], load_sem.at[2 + 2 * part]))
        loads.append(pltpu.make_async_copy(x_hbm.at[:, at], x_v.at[:, at], load_sem.at[3 + 2 * part]))
    for copy in loads:
        copy.start()

    barrier = pltpu.get_barrier_semaphore()
    for dz in (4, 3, 5, 2, 6, 1, 7):
        pl.semaphore_signal(barrier, inc=1, device_id=(z_peer(dz),), device_id_type=MESH)
    for dy, dx in PLANE:
        pl.semaphore_signal(barrier, inc=1, device_id=(plane_peer(dy, dx),), device_id_type=MESH)
    pl.semaphore_signal(barrier, inc=1, device_id=(partner,), device_id_type=MESH)

    for copy in loads[0:2]:
        copy.wait()
    q2 = jnp.concatenate(split(q_v[...], 2), axis=0)
    gq2 = jnp.concatenate(split(fold(nt(q2, g_v[...])) * (1.0 / 16.0), 2), axis=0)

    def term(part):
        for copy in loads[2 + 2 * part : 4 + 2 * part]:
            copy.wait()
        for c in range(part * PART // CH, (part + 1) * PART // CH):
            at = pl.ds(c * CH, CH)
            v = fold(nt(q2, f_v[at, :]) + nn(gq2, x_v[:, at]))
            for i in range(4):
                terms[c * 4 + i] = v[:, i * 128 : (i + 1) * 128]

    def to_core(part):
        at = pl.ds(part * BLOCKS, BLOCKS)
        send(terms.at[at, other], core_recv.at[at], send_sem.at[0], core_sem.at[part], partner)

    def piece(part, to):
        return part * BLOCKS + lax.div(to, 2), pl.ds(pl.multiple_of(lax.rem(to, 2) * ROWS, ROWS), ROWS)

    def to_plane(part):
        at = pl.ds(part * BLOCKS, BLOCKS)
        take(core_recv.at[at], core_sem.at[part])
        acc[at] = terms[at, own, :] + core_recv[at]
        for dy, dx in PLANE:
            send(
                acc.at[piece(part, place(dy, dx))], plane_recv.at[part, dy * 4 + dx],
                send_sem.at[1], plane_sem.at[part], plane_peer(dy, dx),
            )

    term(0)
    pl.semaphore_wait(barrier, 23)
    to_core(0)
    term(1)
    to_core(1)
    term(2)
    to_core(2)
    to_plane(0)
    term(3)
    to_core(3)
    for part in range(1, PARTS):
        to_plane(part)

    for part in range(PARTS):
        for c in range(part * PART // CH, (part + 1) * PART // CH):
            at = pl.ds(c * CH, CH)
            m_ref[at, :] = tn(x_v[:, at], g_v[...]) * (1.0 / 16.0) + f_v[at, :].astype(F32)
        at = pl.ds(part * PART, PART)
        send(m_ref.at[at], m_peer.at[at], send_sem.at[8], peer_sem.at[part], partner)

    def chip(part):
        at = pl.ds(part * PART, PART)
        take(m_peer.at[at], peer_sem.at[part])
        m1, m2 = split(m_ref[at, :] + m_peer[at, :], 2)
        m_chip[0, at, :] = m1
        m_chip[1, at, :] = m2

    for part in range(PARTS):
        if part == 3:
            pass
        take(plane_recv.at[part, pl.ds(1, 15)], plane_sem.at[part])
        block, rows = piece(part, plane)
        s = acc[block, rows, :]
        for d in range(1, 16):
            s = s + plane_recv[part, d]
        z_group[part, z] = s
        mine = z_group.at[part, z]
        for dz in range(1, 8):
            send(mine, mine, send_sem.at[2], z_sem.at[part], z_peer(dz))

    chip(0)
    chip(1)
    for part in range(PARTS):
        if part == 3:
            pass
        take(z_group.at[part, pl.ds(0, 7)], z_sem.at[part])
        s = z_group[part, 0]
        for k in range(1, 8):
            s = s + z_group[part, k]
        block = part * BLOCKS + lax.div(plane, 2)
        rows = pl.ds(pl.multiple_of(core * HALF + lax.rem(plane, 2) * ROWS, ROWS), ROWS)
        p_full[block, rows, :] = s
        mine = p_full.at[block, rows]
        for dy, dx in PLANE:
            send(mine, mine, send_sem.at[3], gather_sem.at[part], plane_peer(dy, dx))

    def pieces(c, count):
        p = p_full[pl.ds(c * 4, 4)]
        p = jnp.concatenate([p[i] for i in range(4)], axis=1)
        return jnp.concatenate(split(p, count), axis=0)

    def consume(part):
        blocks = p_full[pl.ds(part * BLOCKS, BLOCKS), own, :]
        near, far = [], []
        for c in range(PART // CH):
            p = jnp.concatenate([blocks[c * 4 + i] for i in range(4)], axis=1)
            p1, p2 = split(p, 2)
            at = pl.ds(part * PART + c * CH, CH)
            near.append(nn(jnp.concatenate([p1, p2], axis=0), m_chip[0, at, :]))
            far.append(nn(p1, m_chip[1, at, :]))
        near, far = sum(near[1:], near[0]), sum(far[1:], far[0])
        total = (far + near[HALF:]) + near[:HALF]
        st_v[...] = total if part == 0 else st_v[...] + total

    def forward(part):
        take(plane_recv.at[part, pl.ds(1, 15)], gather_sem.at[part])
        rows = p_full.at[pl.ds(part * BLOCKS, BLOCKS), own]
        send(rows, rows, send_sem.at[4], pair_sem.at[part], partner)

    chip(2)
    chip(3)
    for part in range(PARTS):
        forward(part)
        consume(part)

    s = st_v[...]
    for p in range(16):
        s_send[p] = s[(p // 4) * 8 : (p // 4) * 8 + 8, (p % 4) * 128 : (p % 4) * 128 + 128]
    for dy, dx in PLANE:
        send(
            s_send.at[place(dy, dx)], s_recv.at[dy * 4 + dx],
            send_sem.at[5], s_sem.at[0], plane_peer(dy, dx),
        )

    for part in range(PARTS):
        take(p_full.at[pl.ds(part * BLOCKS, BLOCKS), own], pair_sem.at[part])
    gram = jnp.zeros((3 * RANK, 3 * RANK), F32)
    for c in range(8):
        p3 = pieces(c, 3)
        gram = gram + nt(p3, p3)
        pt_ref[c * CH : (c + 1) * CH, :] = p3[0:128].T
    gram = fold(gram)
    gram = (gram[:, 128:192] + gram[:, 64:128]) + gram[:, 0:64]
    rows = lax.broadcasted_iota(jnp.int32, (RANK, RANK), 0)
    cols = lax.broadcasted_iota(jnp.int32, (RANK, RANK), 1)
    eye = (rows == cols).astype(F32)
    a = jnp.concatenate([gram, eye], axis=1)
    a = eliminate(a, 0, 8)

    take(s_recv.at[pl.ds(1, 15)], s_sem.at[0])
    s = s_send[plane]
    for d in range(1, 16):
        s = s + s_recv[d]
    s_group[z] = s
    mine = s_group.at[z]
    for dz in range(1, 8):
        send(mine, mine, send_sem.at[6], s_sem.at[1], z_peer(dz))
    a = eliminate(a, 8, 36)
    take(s_group.at[pl.ds(0, 7)], s_sem.at[1])
    s = s_group[0]
    for k in range(1, 8):
        s = s + s_group[k]
    tile = core * 16 + plane
    s_full[tile] = s
    mine = s_full.at[tile]
    for dy, dx in PLANE:
        send(mine, mine, send_sem.at[7], s_sem.at[2], plane_peer(dy, dx))
        send(mine, mine, send_sem.at[7], s_sem.at[2], plane_peer(dy, dx) + partner - me)
    send(mine, mine, send_sem.at[7], s_sem.at[2], partner)
    a = eliminate(a, 36, 64)
    diag = jnp.sum(a[:, 0:64] * eye, axis=1, keepdims=True)
    inv = a[:, 64:128] * (1.0 / jnp.sqrt(diag))
    inv_t = inv.T
    take(core_recv, send_sem.at[0])
    take(plane_recv.at[:, pl.ds(1, 15)], send_sem.at[1])
    take(z_group.at[:, pl.ds(0, 7)], send_sem.at[2])
    take(plane_recv.at[:, pl.ds(1, 15)], send_sem.at[3])
    take(core_recv, send_sem.at[4])
    take(s_recv.at[pl.ds(1, 15)], send_sem.at[5])
    take(s_group.at[pl.ds(0, 7)], send_sem.at[6])
    take(m_peer, send_sem.at[8])
    take(s_full.at[pl.ds(0, 31)], s_sem.at[2])

    s = jnp.concatenate(
        [jnp.concatenate([s_full[4 * r + i] for i in range(4)], axis=1) for r in range(8)],
        axis=0,
    )
    qn = jnp.dot(inv, s, precision=HIGH, preferred_element_type=F32) * (1.0 / N_DP)
    w = jnp.dot(inv_t, qn, precision=HIGH, preferred_element_type=F32)
    w1, w2 = split(w, 2)
    w = jnp.concatenate([w1, w1, w2, w2], axis=0)
    w_ref[...] = w
    qn_ref[...] = qn
    p = pt_ref[pl.ds(pl.multiple_of(me * 16, 16), 16), :]
    upd_ref[...] = nn(jnp.concatenate([p, p], axis=1), w)
    take(s_full.at[pl.ds(0, 31)], send_sem.at[7])


def finish(upd_v, qn_v, m_v, pt_v, w_v, upd_hbm, qn_hbm, out_hbm, out_v, small_sem):
    small = [
        pltpu.make_async_copy(upd_v, upd_hbm, small_sem.at[0]),
        pltpu.make_async_copy(qn_v, qn_hbm, small_sem.at[1]),
    ]
    for copy in small:
        copy.start()
    w = w_v[...]
    for i in range(D // CH):
        at = pl.ds(i * CH, CH)
        p = pt_v[at, :]
        out_v[at, :] = (m_v[at, :] - nn(jnp.concatenate([p, p], axis=1), w)).astype(BF16)
        pltpu.make_async_copy(out_v.at[at, :], out_hbm.at[at, :], small_sem.at[2]).start()
    for copy in small:
        copy.wait()
    pltpu.make_async_copy(out_v, out_hbm, small_sem.at[2]).wait()


def body(inputs, out_grads, feedback, q_start):
    dma = pltpu.SemaphoreType.DMA
    vmem = pltpu.VMEM
    in_vmem = pl.BlockSpec(memory_space=vmem)
    in_any = pl.BlockSpec(memory_space=pl.ANY)
    upd, qn, m, pt, w = pl.pallas_call(
        kernel,
        out_shape=(
            vmem((D // N_DP, KV), F32),
            vmem((RANK, KV), F32),
            vmem((D, KV), F32),
            vmem((D, 128), BF16),
            vmem((256, KV), BF16),
        ),
        in_specs=[in_any] * 4,
        out_specs=(in_vmem,) * 5,
        scratch_shapes=[
            vmem((TOK, D), BF16),
            vmem((TOK, KV), BF16),
            vmem((D, KV), BF16),
            vmem((RANK, KV), F32),
            vmem((32, RANK, 128), F32),
            vmem((32, RANK, 128), F32),
            vmem((32, HALF, 128), F32),
            vmem((32, HALF, 128), F32),
            vmem((PARTS, 16, ROWS, 128), F32),
            vmem((PARTS, 8, ROWS, 128), F32),
            vmem((D, KV), F32),
            vmem((2, D, KV), BF16),
            vmem((HALF, KV), F32),
            vmem((16, 8, 128), F32),
            vmem((16, 8, 128), F32),
            vmem((8, 8, 128), F32),
            vmem((32, 8, 128), F32),
            dma((2 + 2 * PARTS,)), dma((9,)), dma((PARTS,)), dma((PARTS,)),
            dma((PARTS,)), dma((PARTS,)), dma((PARTS,)), dma((3,)), dma((PARTS,)),
        ],
        compiler_params=pltpu.CompilerParams(
            collective_id=0, has_side_effects=True, vmem_limit_bytes=52 * MIB
        ),
    )(inputs, out_grads, feedback, q_start.T)
    upd, qn, new_feedback = pl.pallas_call(
        finish,
        out_shape=(
            jax.ShapeDtypeStruct((D // N_DP, KV), F32),
            jax.ShapeDtypeStruct((RANK, KV), F32),
            jax.ShapeDtypeStruct((D, KV), BF16),
        ),
        in_specs=[in_vmem] * 5,
        out_specs=(in_any,) * 3,
        scratch_shapes=[vmem((D, KV), BF16), dma((3,))],
        compiler_params=pltpu.CompilerParams(vmem_limit_bytes=16 * MIB),
    )(upd, qn, m, pt, w)
    return upd, qn.T, new_feedback


def solution(mesh):
    placed = (P("dp", None), P("dp", None), P("dp", None), P())
    return jax.shard_map(
        body,
        mesh=mesh,
        in_specs=placed,
        out_specs=(P("dp", None), P(), P("dp", None)),
        check_vma=False,
    )
```

```python
import jax
import jax.numpy as jnp
from jax import lax
from jax.experimental import pallas as pl
from jax.experimental.pallas import tpu as pltpu
from jax.sharding import PartitionSpec as P

HIGH = lax.Precision.HIGHEST
MESH = pl.DeviceIdType.MESH
F32, BF16 = jnp.float32, jnp.bfloat16

D, KV, RANK, TOK, N_DP = 4096, 512, 64, 256, 256
HALF = RANK // 2
CH = 512
CHUNKS = (2, 2, 2, 2)
PARTS = len(CHUNKS)
FIRST = [sum(CHUNKS[:part]) for part in range(PARTS)]
MPARTS = 4
MPART = D // MPARTS
PLANE = [(2, 2), (2, 1), (2, 3), (1, 2), (3, 2), (1, 1), (1, 3), (3, 1), (3, 3), (2, 0), (0, 2), (0, 1), (0, 3), (1, 0), (3, 0)]
MIB = 1024 * 1024


def nn(a, b):
    return lax.dot_general(a, b, (((1,), (0,)), ((), ())), preferred_element_type=F32)


def nt(a, b):
    return lax.dot_general(a, b, (((1,), (1,)), ((), ())), preferred_element_type=F32)


def tn(a, b):
    return lax.dot_general(a, b, (((0,), (0,)), ((), ())), preferred_element_type=F32)


def split(v, pieces):
    out = []
    for at in range(pieces):
        out.append(v.astype(BF16))
        if at < pieces - 1:
            v = v - out[-1].astype(F32)
    return out


def fold(t):
    out = t[-RANK:]
    for at in range(t.shape[0] - 2 * RANK, -1, -RANK):
        out = out + t[at : at + RANK]
    return out


def eliminate(a, first, last):
    rows = lax.broadcasted_iota(jnp.int32, (RANK, 1), 0)
    for k in range(first, last):
        row = a[k : k + 1, :]
        ratio = a[:, k : k + 1] / a[k : k + 1, k : k + 1]
        a = a - jnp.where(rows > k, ratio, 0.0) * row
    return a


def kernel(
    x_hbm, g_hbm, f_hbm, q_hbm, upd_ref, qn_ref, m_ref, pt_ref, w_ref,
    x_v, g_v, f_v, q_v, p_full,
    terms, core_recv, acc, plane_recv, z_group,
    m_peer, m_chip, st_v, s_send, s_recv, s_group, s_full,
    load_sem, send_sem, core_sem, plane_sem, z_sem, gather_sem, pair_sem, s_sem, peer_sem,
):
    me = lax.axis_index("dp")
    core = lax.rem(me, 2)
    z = lax.rem(lax.div(me, 2), 8)
    group = lax.rem(me, 16)
    plane = lax.div(me, 16)
    y, x = lax.div(plane, 4), lax.rem(plane, 4)
    partner = me + 1 - 2 * core
    own = pl.ds(pl.multiple_of(core * HALF, HALF), HALF)
    other = pl.ds(pl.multiple_of((1 - core) * HALF, HALF), HALF)

    def place(dy, dx):
        return lax.rem(y + dy, 4) * 4 + lax.rem(x + dx, 4)

    def plane_peer(dy, dx):
        return place(dy, dx) * 16 + group

    def z_peer(dz):
        return plane * 16 + lax.rem(z + dz, 8) * 2 + core

    def send(src, dst, ss, rs, device):
        pltpu.make_async_remote_copy(
            src_ref=src, dst_ref=dst, send_sem=ss, recv_sem=rs,
            device_id=(device,), device_id_type=MESH,
        ).start()

    def take(like, sem):
        pltpu.make_async_copy(like, like, sem).wait()

    def span(part):
        return pl.ds(FIRST[part] * CH, CHUNKS[part] * CH)

    def blocks(part):
        return pl.ds(FIRST[part] * 4, CHUNKS[part] * 4)

    def rows_of(part):
        return 8 * CHUNKS[part]

    def piece(part, to, base):
        rows = rows_of(part)
        per = HALF // rows
        block = FIRST[part] * 4 + lax.div(to, per)
        return block, pl.ds(pl.multiple_of(base + lax.rem(to, per) * rows, 8), rows)

    def slots(ref, part, first, count):
        return ref.at[part, pl.ds(first, count), pl.ds(0, rows_of(part))]

    loads = [
        pltpu.make_async_copy(q_hbm, q_v, load_sem.at[0]),
        pltpu.make_async_copy(g_hbm, g_v, load_sem.at[1]),
    ]
    for part in range(PARTS):
        at = span(part)
        loads.append(pltpu.make_async_copy(f_hbm.at[at, :], f_v.at[at, :], load_sem.at[2 + 2 * part]))
        loads.append(pltpu.make_async_copy(x_hbm.at[:, at], x_v.at[:, at], load_sem.at[3 + 2 * part]))
    for copy in loads:
        copy.start()

    barrier = pltpu.get_barrier_semaphore()
    for dz in (4, 3, 5, 2, 6, 1, 7):
        pl.semaphore_signal(barrier, inc=1, device_id=(z_peer(dz),), device_id_type=MESH)
    for dy, dx in PLANE:
        pl.semaphore_signal(barrier, inc=1, device_id=(plane_peer(dy, dx),), device_id_type=MESH)
    pl.semaphore_signal(barrier, inc=1, device_id=(partner,), device_id_type=MESH)

    for copy in loads[0:2]:
        copy.wait()
    q2 = jnp.concatenate(split(q_v[...], 2), axis=0)
    gq2 = jnp.concatenate(split(fold(nt(q2, g_v[...])) * (1.0 / 16.0), 2), axis=0)

    def term(part):
        for copy in loads[2 + 2 * part : 4 + 2 * part]:
            copy.wait()
        for c in range(FIRST[part], FIRST[part] + CHUNKS[part]):
            at = pl.ds(c * CH, CH)
            v = fold(nt(q2, f_v[at, :]) + nn(gq2, x_v[:, at]))
            for i in range(4):
                terms[c * 4 + i] = v[:, i * 128 : (i + 1) * 128]

    def to_core(part):
        at = blocks(part)
        send(terms.at[at, other], core_recv.at[at], send_sem.at[0], core_sem.at[part], partner)

    def to_plane(part):
        at = blocks(part)
        take(core_recv.at[at], core_sem.at[part])
        acc[at] = terms[at, own, :] + core_recv[at]
        for dy, dx in PLANE:
            send(
                acc.at[piece(part, place(dy, dx), 0)],
                plane_recv.at[part, dy * 4 + dx, pl.ds(0, rows_of(part))],
                send_sem.at[1], plane_sem.at[part], plane_peer(dy, dx),
            )

    def matrix(part):
        at = pl.ds(part * MPART, MPART)
        for c in range(part * MPART // CH, (part + 1) * MPART // CH):
            rows = pl.ds(c * CH, CH)
            m_ref[rows, :] = tn(x_v[:, rows], g_v[...]) * (1.0 / 16.0) + f_v[rows, :].astype(F32)
        send(m_ref.at[at], m_peer.at[at], send_sem.at[8], peer_sem.at[part], partner)

    term(0)
    pl.semaphore_wait(barrier, 23)
    to_core(0)
    for part in range(1, PARTS):
        term(part)
        to_core(part)
        if part >= 2:
            to_plane(part - 2)
    matrix(0)
    to_plane(PARTS - 2)
    matrix(1)
    to_plane(PARTS - 1)
    take(core_recv, send_sem.at[0])
    for part in range(2, MPARTS):
        matrix(part)

    def chip(part):
        at = pl.ds(part * MPART, MPART)
        take(m_peer.at[at], peer_sem.at[part])
        m1, m2 = split(m_ref[at, :] + m_peer[at, :], 2)
        m_chip[0, at, :] = m1
        m_chip[1, at, :] = m2

    for part in range(PARTS):
        if part == PARTS - 1:
            pass
        take(slots(plane_recv, part, 1, 15), plane_sem.at[part])
        rows = pl.ds(0, rows_of(part))
        block, at = piece(part, plane, 0)
        s = acc[block, at, :]
        for d in range(1, 16):
            s = s + plane_recv[part, d, rows, :]
        z_group[part, z, rows, :] = s
        mine = z_group.at[part, z, rows]
        for dz in range(1, 8):
            send(mine, mine, send_sem.at[2], z_sem.at[part], z_peer(dz))

    chip(0)
    chip(1)
    for part in range(PARTS):
        if part == PARTS - 1:
            pass
        take(slots(z_group, part, 0, 7), z_sem.at[part])
        rows = pl.ds(0, rows_of(part))
        s = z_group[part, 0, rows, :]
        for k in range(1, 8):
            s = s + z_group[part, k, rows, :]
        block, at = piece(part, plane, core * HALF)
        p_full[block, at, :] = s
        mine = p_full.at[block, at]
        for dy, dx in PLANE:
            send(mine, mine, send_sem.at[3], gather_sem.at[part], plane_peer(dy, dx))

    def pieces(c, count):
        p = p_full[pl.ds(c * 4, 4)]
        p = jnp.concatenate([p[i] for i in range(4)], axis=1)
        return jnp.concatenate(split(p, count), axis=0)

    def consume(part):
        held = p_full[blocks(part), own, :]
        near, far = [], []
        for c in range(CHUNKS[part]):
            p = jnp.concatenate([held[c * 4 + i] for i in range(4)], axis=1)
            p1, p2 = split(p, 2)
            at = pl.ds((FIRST[part] + c) * CH, CH)
            near.append(nn(jnp.concatenate([p1, p2], axis=0), m_chip[0, at, :]))
            far.append(nn(p1, m_chip[1, at, :]))
        near, far = sum(near[1:], near[0]), sum(far[1:], far[0])
        total = (far + near[HALF:]) + near[:HALF]
        st_v[...] = total if part == 0 else st_v[...] + total

    def forward(part):
        take(slots(plane_recv, part, 1, 15), gather_sem.at[part])
        rows = p_full.at[blocks(part), own]
        send(rows, rows, send_sem.at[4], pair_sem.at[part], partner)
        if part >= PARTS - 4:
            ref, sem = (
                (core_recv.at[pl.ds(0, 30)], 1), (core_recv.at[pl.ds(0, 14)], 2),
                (m_peer, 8), (core_recv.at[pl.ds(0, 30)], 3),
            )[part - PARTS + 4]
            take(ref, send_sem.at[sem])

    chip(2)
    for part in range(PARTS):
        forward(part)
        consume(part)
        if FIRST[part + 1 : part + 2] == [4]:
            chip(3)

    s = st_v[...]
    for p in range(16):
        s_send[p] = s[(p // 4) * 8 : (p // 4) * 8 + 8, (p % 4) * 128 : (p % 4) * 128 + 128]
    for dy, dx in PLANE:
        send(
            s_send.at[place(dy, dx)], s_recv.at[dy * 4 + dx],
            send_sem.at[5], s_sem.at[0], plane_peer(dy, dx),
        )

    for part in range(PARTS):
        take(p_full.at[blocks(part), own], pair_sem.at[part])
    gram = jnp.zeros((3 * RANK, 3 * RANK), F32)
    for c in range(8):
        p3 = pieces(c, 3)
        gram = gram + nt(p3, p3)
        pt_ref[c * CH : (c + 1) * CH, :] = p3[0:128].T
    gram = fold(gram)
    gram = (gram[:, 128:192] + gram[:, 64:128]) + gram[:, 0:64]
    rows = lax.broadcasted_iota(jnp.int32, (RANK, RANK), 0)
    cols = lax.broadcasted_iota(jnp.int32, (RANK, RANK), 1)
    eye = (rows == cols).astype(F32)
    a = jnp.concatenate([gram, eye], axis=1)
    a = eliminate(a, 0, 8)

    take(s_recv.at[pl.ds(1, 15)], s_sem.at[0])
    s = s_send[plane]
    for d in range(1, 16):
        s = s + s_recv[d]
    s_group[core, z] = s
    mine = s_group.at[core, z]
    for dz in (4, 3, 5, 2, 6, 1, 7):
        send(mine, mine, send_sem.at[6], s_sem.at[1], z_peer(dz))
        send(mine, mine, send_sem.at[6], s_sem.at[1], z_peer(dz) + partner - me)
    send(mine, mine, send_sem.at[6], s_sem.at[1], partner)
    take(core_recv, send_sem.at[4])
    a = eliminate(a, 8, 36)
    take(s_recv.at[pl.ds(1, 15)], s_sem.at[1])
    s = s_group[:, 0]
    for k in range(1, 8):
        s = s + s_group[:, k]
    s_full[plane] = s
    mine = s_full.at[plane]
    for dy, dx in PLANE:
        send(mine, mine, send_sem.at[7], s_sem.at[2], plane_peer(dy, dx))
    take(s_recv.at[pl.ds(1, 15)], send_sem.at[5])
    a = eliminate(a, 36, 64)
    diag = jnp.sum(a[:, 0:64] * eye, axis=1, keepdims=True)
    inv = a[:, 64:128] * (1.0 / jnp.sqrt(diag))
    inv_t = inv.T
    take(s_full.at[pl.ds(1, 15)], s_sem.at[2])

    s = jnp.concatenate(
        [
            jnp.concatenate([s_full[4 * r + i, half] for i in range(4)], axis=1)
            for half in range(2)
            for r in range(4)
        ],
        axis=0,
    )
    qn = jnp.dot(inv, s, precision=HIGH, preferred_element_type=F32) * (1.0 / N_DP)
    w = jnp.dot(inv_t, qn, precision=HIGH, preferred_element_type=F32)
    w1, w2 = split(w, 2)
    w = jnp.concatenate([w1, w1, w2, w2], axis=0)
    w_ref[...] = w
    qn_ref[...] = qn
    p = pt_ref[pl.ds(pl.multiple_of(me * 16, 16), 16), :]
    upd_ref[...] = nn(jnp.concatenate([p, p], axis=1), w)
    take(s_recv.at[pl.ds(1, 15)], send_sem.at[6])
    take(s_full.at[pl.ds(1, 15)], send_sem.at[7])


def finish(upd_v, qn_v, m_v, pt_v, w_v, upd_hbm, qn_hbm, out_hbm, out_v, small_sem):
    small = [
        pltpu.make_async_copy(upd_v, upd_hbm, small_sem.at[0]),
        pltpu.make_async_copy(qn_v, qn_hbm, small_sem.at[1]),
    ]
    for copy in small:
        copy.start()
    w = w_v[...]
    for i in range(D // CH):
        at = pl.ds(i * CH, CH)
        p = pt_v[at, :]
        out_v[at, :] = (m_v[at, :] - nn(jnp.concatenate([p, p], axis=1), w)).astype(BF16)
        pltpu.make_async_copy(out_v.at[at, :], out_hbm.at[at, :], small_sem.at[2]).start()
    for copy in small:
        copy.wait()
    pltpu.make_async_copy(out_v, out_hbm, small_sem.at[2]).wait()


def body(inputs, out_grads, feedback, q_start):
    dma = pltpu.SemaphoreType.DMA
    vmem = pltpu.VMEM
    in_vmem = pl.BlockSpec(memory_space=vmem)
    in_any = pl.BlockSpec(memory_space=pl.ANY)
    upd, qn, m, pt, w = pl.pallas_call(
        kernel,
        out_shape=(
            vmem((D // N_DP, KV), F32),
            vmem((RANK, KV), F32),
            vmem((D, KV), F32),
            vmem((D, 128), BF16),
            vmem((256, KV), BF16),
        ),
        in_specs=[in_any] * 4,
        out_specs=(in_vmem,) * 5,
        scratch_shapes=[
            vmem((TOK, D), BF16),
            vmem((TOK, KV), BF16),
            vmem((D, KV), BF16),
            vmem((RANK, KV), F32),
            vmem((32, RANK, 128), F32),
            vmem((32, RANK, 128), F32),
            vmem((32, HALF, 128), F32),
            vmem((32, HALF, 128), F32),
            vmem((PARTS, 16, 8 * max(CHUNKS), 128), F32),
            vmem((PARTS, 8, 8 * max(CHUNKS), 128), F32),
            vmem((D, KV), F32),
            vmem((2, D, KV), BF16),
            vmem((HALF, KV), F32),
            vmem((16, 8, 128), F32),
            vmem((16, 8, 128), F32),
            vmem((2, 8, 8, 128), F32),
            vmem((16, 2, 8, 128), F32),
            dma((2 + 2 * PARTS,)), dma((9,)), dma((PARTS,)), dma((PARTS,)),
            dma((PARTS,)), dma((PARTS,)), dma((PARTS,)), dma((3,)), dma((MPARTS,)),
        ],
        compiler_params=pltpu.CompilerParams(
            collective_id=0, has_side_effects=True, vmem_limit_bytes=52 * MIB
        ),
    )(inputs, out_grads, feedback, q_start.T)
    upd, qn, new_feedback = pl.pallas_call(
        finish,
        out_shape=(
            jax.ShapeDtypeStruct((D // N_DP, KV), F32),
            jax.ShapeDtypeStruct((RANK, KV), F32),
            jax.ShapeDtypeStruct((D, KV), BF16),
        ),
        in_specs=[in_vmem] * 5,
        out_specs=(in_any,) * 3,
        scratch_shapes=[vmem((D, KV), BF16), dma((3,))],
        compiler_params=pltpu.CompilerParams(vmem_limit_bytes=16 * MIB),
    )(upd, qn, m, pt, w)
    return upd, qn.T, new_feedback


def solution(mesh):
    placed = (P("dp", None), P("dp", None), P("dp", None), P())
    return jax.shard_map(
        body,
        mesh=mesh,
        in_specs=placed,
        out_specs=(P("dp", None), P(), P("dp", None)),
        check_vma=False,
    )
```

```python
import jax
import jax.numpy as jnp
from jax import lax
from jax.experimental import pallas as pl
from jax.experimental.pallas import tpu as pltpu
from jax.sharding import PartitionSpec as P

MESH = pl.DeviceIdType.MESH
F32, BF16 = jnp.float32, jnp.bfloat16

D, KV, RANK, TOK, N_DP = 4096, 512, 64, 256, 256
HALF = RANK // 2
CH = 512
CHUNKS = (2, 2, 2, 2)
PARTS = len(CHUNKS)
FIRST = [sum(CHUNKS[:part]) for part in range(PARTS)]
MPARTS = 4
MPART = D // MPARTS
PLANE = [(2, 2), (2, 1), (2, 3), (1, 2), (3, 2), (1, 1), (1, 3), (3, 1), (3, 3), (2, 0), (0, 2), (0, 1), (0, 3), (1, 0), (3, 0)]
MIB = 1024 * 1024


def nn(a, b):
    return lax.dot_general(a, b, (((1,), (0,)), ((), ())), preferred_element_type=F32)


def nt(a, b):
    return lax.dot_general(a, b, (((1,), (1,)), ((), ())), preferred_element_type=F32)


def tn(a, b):
    return lax.dot_general(a, b, (((0,), (0,)), ((), ())), preferred_element_type=F32)


def split(v, pieces):
    out = []
    for at in range(pieces):
        out.append(v.astype(BF16))
        if at < pieces - 1:
            v = v - out[-1].astype(F32)
    return out


def fold(t):
    out = t[-RANK:]
    for at in range(t.shape[0] - 2 * RANK, -1, -RANK):
        out = out + t[at : at + RANK]
    return out


def beside(v):
    v1, v2, v3 = split(v, 3)
    return jnp.concatenate([v1, v1, v2, v1, v2, v3], axis=1)


def below(v):
    v1, v2, v3 = split(v, 3)
    return jnp.concatenate([v1, v2, v1, v3, v2, v1], axis=0)


def eliminate(a, first, last):
    rows = lax.broadcasted_iota(jnp.int32, (RANK, 1), 0)
    for k in range(first, last):
        row = a[k : k + 1, :]
        ratio = a[:, k : k + 1] / a[k : k + 1, k : k + 1]
        a = a - jnp.where(rows > k, ratio, 0.0) * row
    return a


def kernel(
    x_hbm, g_hbm, f_hbm, q_hbm, pm_ref, qn_ref, m_ref, pt_ref, w_ref,
    x_v, g_v, f_v, q_v, p_full,
    terms, core_recv, acc, plane_recv, z_group,
    m_peer, m_chip, st_v, s_send, s_recv, s_group, s_full,
    load_sem, send_sem, core_sem, plane_sem, z_sem, gather_sem, pair_sem, s_sem, peer_sem,
):
    me = lax.axis_index("dp")
    core = lax.rem(me, 2)
    z = lax.rem(lax.div(me, 2), 8)
    group = lax.rem(me, 16)
    plane = lax.div(me, 16)
    y, x = lax.div(plane, 4), lax.rem(plane, 4)
    partner = me + 1 - 2 * core
    own = pl.ds(pl.multiple_of(core * HALF, HALF), HALF)
    other = pl.ds(pl.multiple_of((1 - core) * HALF, HALF), HALF)

    def place(dy, dx):
        return lax.rem(y + dy, 4) * 4 + lax.rem(x + dx, 4)

    def plane_peer(dy, dx):
        return place(dy, dx) * 16 + group

    def z_peer(dz):
        return plane * 16 + lax.rem(z + dz, 8) * 2 + core

    def send(src, dst, ss, rs, device):
        pltpu.make_async_remote_copy(
            src_ref=src, dst_ref=dst, send_sem=ss, recv_sem=rs,
            device_id=(device,), device_id_type=MESH,
        ).start()

    def take(like, sem):
        pltpu.make_async_copy(like, like, sem).wait()

    def span(part):
        return pl.ds(FIRST[part] * CH, CHUNKS[part] * CH)

    def blocks(part):
        return pl.ds(FIRST[part] * 4, CHUNKS[part] * 4)

    def rows_of(part):
        return 8 * CHUNKS[part]

    def piece(part, to, base):
        rows = rows_of(part)
        per = HALF // rows
        block = FIRST[part] * 4 + lax.div(to, per)
        return block, pl.ds(pl.multiple_of(base + lax.rem(to, per) * rows, 8), rows)

    def slots(ref, part, first, count):
        return ref.at[part, pl.ds(first, count), pl.ds(0, rows_of(part))]

    loads = [
        pltpu.make_async_copy(q_hbm, q_v, load_sem.at[0]),
        pltpu.make_async_copy(g_hbm, g_v, load_sem.at[1]),
    ]
    for part in range(PARTS):
        at = span(part)
        loads.append(pltpu.make_async_copy(f_hbm.at[at, :], f_v.at[at, :], load_sem.at[2 + 2 * part]))
        loads.append(pltpu.make_async_copy(x_hbm.at[:, at], x_v.at[:, at], load_sem.at[3 + 2 * part]))
    for copy in loads:
        copy.start()

    barrier = pltpu.get_barrier_semaphore()
    for dz in (4, 3, 5, 2, 6, 1, 7):
        pl.semaphore_signal(barrier, inc=1, device_id=(z_peer(dz),), device_id_type=MESH)
    for dy, dx in PLANE:
        pl.semaphore_signal(barrier, inc=1, device_id=(plane_peer(dy, dx),), device_id_type=MESH)
    pl.semaphore_signal(barrier, inc=1, device_id=(partner,), device_id_type=MESH)

    for copy in loads[0:2]:
        copy.wait()
    q2 = jnp.concatenate(split(q_v[...], 2), axis=0)
    gq2 = jnp.concatenate(split(fold(nt(q2, g_v[...])) * (1.0 / 16.0), 2), axis=0)

    def term(part):
        for copy in loads[2 + 2 * part : 4 + 2 * part]:
            copy.wait()
        for c in range(FIRST[part], FIRST[part] + CHUNKS[part]):
            at = pl.ds(c * CH, CH)
            v = fold(nt(q2, f_v[at, :]) + nn(gq2, x_v[:, at]))
            for i in range(4):
                terms[c * 4 + i] = v[:, i * 128 : (i + 1) * 128]

    def to_core(part):
        at = blocks(part)
        send(terms.at[at, other], core_recv.at[at], send_sem.at[0], core_sem.at[part], partner)

    def to_plane(part):
        at = blocks(part)
        take(core_recv.at[at], core_sem.at[part])
        acc[at] = terms[at, own, :] + core_recv[at]
        for dy, dx in PLANE:
            send(
                acc.at[piece(part, place(dy, dx), 0)],
                plane_recv.at[part, dy * 4 + dx, pl.ds(0, rows_of(part))],
                send_sem.at[1], plane_sem.at[part], plane_peer(dy, dx),
            )

    def matrix(part):
        at = pl.ds(part * MPART, MPART)
        for c in range(part * MPART // CH, (part + 1) * MPART // CH):
            rows = pl.ds(c * CH, CH)
            m_ref[rows, :] = tn(x_v[:, rows], g_v[...]) * (1.0 / 16.0) + f_v[rows, :].astype(F32)
        send(m_ref.at[at], m_peer.at[at], send_sem.at[8], peer_sem.at[part], partner)

    term(0)
    pl.semaphore_wait(barrier, 23)
    to_core(0)
    for part in range(1, PARTS):
        term(part)
        to_core(part)
        if part >= 2:
            to_plane(part - 2)
    matrix(0)
    to_plane(PARTS - 2)
    matrix(1)
    to_plane(PARTS - 1)
    take(core_recv, send_sem.at[0])
    for part in range(2, MPARTS):
        matrix(part)

    def chip(part):
        at = pl.ds(part * MPART, MPART)
        take(m_peer.at[at], peer_sem.at[part])
        m1, m2 = split(m_ref[at, :] + m_peer[at, :], 2)
        m_chip[0, at, :] = m1
        m_chip[1, at, :] = m2

    for part in range(PARTS):
        if part == PARTS - 1:
            pass
        take(slots(plane_recv, part, 1, 15), plane_sem.at[part])
        rows = pl.ds(0, rows_of(part))
        block, at = piece(part, plane, 0)
        s = acc[block, at, :]
        for d in range(1, 16):
            s = s + plane_recv[part, d, rows, :]
        z_group[part, z, rows, :] = s
        mine = z_group.at[part, z, rows]
        for dz in (4, 3, 5, 2, 6, 1, 7):
            send(mine, mine, send_sem.at[2], z_sem.at[part], z_peer(dz))

    chip(0)
    chip(1)
    for part in range(PARTS):
        if part == PARTS - 1:
            pass
        take(slots(z_group, part, 0, 7), z_sem.at[part])
        rows = pl.ds(0, rows_of(part))
        s = z_group[part, 0, rows, :]
        for k in range(1, 8):
            s = s + z_group[part, k, rows, :]
        block, at = piece(part, plane, core * HALF)
        p_full[block, at, :] = s
        mine = p_full.at[block, at]
        for dy, dx in PLANE:
            send(mine, mine, send_sem.at[3], gather_sem.at[part], plane_peer(dy, dx))

    def pieces(c, count):
        p = p_full[pl.ds(c * 4, 4)]
        p = jnp.concatenate([p[i] for i in range(4)], axis=1)
        return jnp.concatenate(split(p, count), axis=0)

    def consume(part):
        held = p_full[blocks(part), own, :]
        near, far = [], []
        for c in range(CHUNKS[part]):
            p = jnp.concatenate([held[c * 4 + i] for i in range(4)], axis=1)
            p1, p2 = split(p, 2)
            at = pl.ds((FIRST[part] + c) * CH, CH)
            near.append(nn(jnp.concatenate([p1, p2], axis=0), m_chip[0, at, :]))
            far.append(nn(p1, m_chip[1, at, :]))
        near, far = sum(near[1:], near[0]), sum(far[1:], far[0])
        total = (far + near[HALF:]) + near[:HALF]
        st_v[...] = total if part == 0 else st_v[...] + total

    def forward(part):
        take(slots(plane_recv, part, 1, 15), gather_sem.at[part])
        rows = p_full.at[blocks(part), own]
        send(rows, rows, send_sem.at[4], pair_sem.at[part], partner)
        if part >= PARTS - 4:
            ref, sem = (
                (core_recv.at[pl.ds(0, 30)], 1), (core_recv.at[pl.ds(0, 14)], 2),
                (m_peer, 8), (core_recv.at[pl.ds(0, 30)], 3),
            )[part - PARTS + 4]
            take(ref, send_sem.at[sem])

    chip(2)
    for part in range(PARTS):
        forward(part)
        consume(part)
        if FIRST[part + 1 : part + 2] == [4]:
            chip(3)

    s = st_v[...]
    for p in range(16):
        s_send[p] = s[(p // 4) * 8 : (p // 4) * 8 + 8, (p % 4) * 128 : (p % 4) * 128 + 128]
    for dy, dx in PLANE:
        send(
            s_send.at[place(dy, dx)], s_recv.at[dy * 4 + dx],
            send_sem.at[5], s_sem.at[0], plane_peer(dy, dx),
        )

    take(s_recv.at[pl.ds(1, 15)], s_sem.at[0])
    s = s_send[plane]
    for d in range(1, 16):
        s = s + s_recv[d]
    s_group[core, z] = s
    mine = s_group.at[core, z]
    for dz in (4, 3, 5, 2, 6, 1, 7):
        send(mine, mine, send_sem.at[6], s_sem.at[1], z_peer(dz))
        send(mine, mine, send_sem.at[6], s_sem.at[1], z_peer(dz) + partner - me)
    send(mine, mine, send_sem.at[6], s_sem.at[1], partner)
    take(core_recv, send_sem.at[4])
    for part in range(PARTS):
        take(p_full.at[blocks(part), own], pair_sem.at[part])
    gram = jnp.zeros((3 * RANK, 3 * RANK), F32)
    for c in range(8):
        p3 = pieces(c, 3)
        gram = gram + nt(p3, p3)
        pt_ref[c * CH : (c + 1) * CH, :] = p3[0:128].T
    gram = fold(gram)
    gram = (gram[:, 128:192] + gram[:, 64:128]) + gram[:, 0:64]
    rows = lax.broadcasted_iota(jnp.int32, (RANK, RANK), 0)
    cols = lax.broadcasted_iota(jnp.int32, (RANK, RANK), 1)
    eye = (rows == cols).astype(F32)
    a = jnp.concatenate([gram, eye], axis=1)
    a = eliminate(a, 0, 24)

    take(s_recv.at[pl.ds(1, 15)], s_sem.at[1])
    s = s_group[:, 0]
    for k in range(1, 8):
        s = s + s_group[:, k]
    s_full[plane] = s
    mine = s_full.at[plane]
    for dy, dx in PLANE:
        send(mine, mine, send_sem.at[7], s_sem.at[2], plane_peer(dy, dx))
    take(s_recv.at[pl.ds(1, 15)], send_sem.at[5])
    a = eliminate(a, 24, 64)
    diag = jnp.sum(a[:, 0:64] * eye, axis=1, keepdims=True)
    inv = a[:, 64:128] * (1.0 / jnp.sqrt(diag))
    left, left_t = beside(inv), beside(inv.T)
    pm_ref[...] = pt_ref[pl.ds(pl.multiple_of(me * 16, 16), 16), :]
    take(s_full.at[pl.ds(1, 15)], s_sem.at[2])

    s = jnp.concatenate(
        [
            jnp.concatenate([s_full[4 * r + i, half] for i in range(4)], axis=1)
            for half in range(2)
            for r in range(4)
        ],
        axis=0,
    )
    qn = nn(left, below(s)) * (1.0 / N_DP)
    w = nn(left_t, below(qn))
    w1, w2 = split(w, 2)
    w = jnp.concatenate([w1, w1, w2, w2], axis=0)
    w_ref[...] = w
    qn_ref[...] = qn
    take(s_recv.at[pl.ds(1, 15)], send_sem.at[6])
    take(s_full.at[pl.ds(1, 15)], send_sem.at[7])


def finish(pm_v, qn_v, m_v, pt_v, w_v, upd_hbm, qn_hbm, out_hbm, out_v, upd_v, sem):
    copies = [
        pltpu.make_async_copy(qn_v, qn_hbm, sem.at[0]),
        pltpu.make_async_copy(upd_v, upd_hbm, sem.at[1]),
    ]
    copies[0].start()
    w = w_v[...]
    for i in range(D // CH):
        at = pl.ds(i * CH, CH)
        p = pt_v[at, :]
        out_v[at, :] = (m_v[at, :] - nn(jnp.concatenate([p, p], axis=1), w)).astype(BF16)
        pltpu.make_async_copy(out_v.at[at, :], out_hbm.at[at, :], sem.at[2]).start()
    p = pm_v[...]
    upd_v[...] = nn(jnp.concatenate([p, p], axis=1), w)
    copies[1].start()
    for copy in copies:
        copy.wait()
    pltpu.make_async_copy(out_v, out_hbm, sem.at[2]).wait()


def body(inputs, out_grads, feedback, q_start):
    dma = pltpu.SemaphoreType.DMA
    vmem = pltpu.VMEM
    in_vmem = pl.BlockSpec(memory_space=vmem)
    in_any = pl.BlockSpec(memory_space=pl.ANY)
    pm, qn, m, pt, w = pl.pallas_call(
        kernel,
        out_shape=(
            vmem((D // N_DP, 128), BF16),
            vmem((RANK, KV), F32),
            vmem((D, KV), F32),
            vmem((D, 128), BF16),
            vmem((256, KV), BF16),
        ),
        in_specs=[in_any] * 4,
        out_specs=(in_vmem,) * 5,
        scratch_shapes=[
            vmem((TOK, D), BF16),
            vmem((TOK, KV), BF16),
            vmem((D, KV), BF16),
            vmem((RANK, KV), F32),
            vmem((32, RANK, 128), F32),
            vmem((32, RANK, 128), F32),
            vmem((32, HALF, 128), F32),
            vmem((32, HALF, 128), F32),
            vmem((PARTS, 16, 8 * max(CHUNKS), 128), F32),
            vmem((PARTS, 8, 8 * max(CHUNKS), 128), F32),
            vmem((D, KV), F32),
            vmem((2, D, KV), BF16),
            vmem((HALF, KV), F32),
            vmem((16, 8, 128), F32),
            vmem((16, 8, 128), F32),
            vmem((2, 8, 8, 128), F32),
            vmem((16, 2, 8, 128), F32),
            dma((2 + 2 * PARTS,)), dma((9,)), dma((PARTS,)), dma((PARTS,)),
            dma((PARTS,)), dma((PARTS,)), dma((PARTS,)), dma((3,)), dma((MPARTS,)),
        ],
        compiler_params=pltpu.CompilerParams(
            collective_id=0, has_side_effects=True, vmem_limit_bytes=52 * MIB
        ),
    )(inputs, out_grads, feedback, q_start.T)
    upd, qn, new_feedback = pl.pallas_call(
        finish,
        out_shape=(
            jax.ShapeDtypeStruct((D // N_DP, KV), F32),
            jax.ShapeDtypeStruct((RANK, KV), F32),
            jax.ShapeDtypeStruct((D, KV), BF16),
        ),
        in_specs=[in_vmem] * 5,
        out_specs=(in_any,) * 3,
        scratch_shapes=[vmem((D, KV), BF16), vmem((D // N_DP, KV), F32), dma((3,))],
        compiler_params=pltpu.CompilerParams(vmem_limit_bytes=16 * MIB),
    )(pm, qn, m, pt, w)
    return upd, qn.T, new_feedback


def solution(mesh):
    placed = (P("dp", None), P("dp", None), P("dp", None), P())
    return jax.shard_map(
        body,
        mesh=mesh,
        in_specs=placed,
        out_specs=(P("dp", None), P(), P("dp", None)),
        check_vma=False,
    )
```
